32 devices in a mesh: gx: 8 (over z, y), gy: 4 (over x, core).
Axes of the slice: x: 2, y: 2, z: 4, core: 2. Of those that a mesh axis runs over, the one named last changes fastest.
Arguments:
- rate_x: float32 [40, 64, 512], P(None, 'gx', 'gy'), may hold values from 0.0025 to 0.25
- rate_y: float32 [40, 64, 512], P(None, 'gx', 'gy'), may hold values from 0.00015625 to 0.015625
- land_mask: int32 [64, 512], P('gx', 'gy'), may hold values 0 or 1
- obs_cell: int32 [32, 32, 32], P(('gx', 'gy')), may hold values from 0 to 81919
- obs_count: int32 [32, 32], P(('gx', 'gy')), may hold values from 0 to 32, as said below
- innovation: float32 [32, 32, 32], P(('gx', 'gy')), may hold values from -12 to 12
- obs_weight: float32 [32, 4, 256, 256], P(('gx', 'gy')), may hold values from -9 to 9, as said below
Outputs:
- solution: float32 [2, 40, 64, 512], P(None, None, 'gx', 'gy')
- residual: float32 [2, 40, 64, 512], P(None, None, 'gx', 'gy')
The draws below stay inside these ranges and needn't reach their ends.
Inputs may be any that keep to these rules, and one draw needn't show every extreme that they name: obs_count[s, d] slots of pair (s, d) hold observations, slots 0 to obs_count[s, d] - 1; in every draw some owner d has obs_count[s, d] = 32 for every source s. Each block obs_weight[s, n] is symmetric positive definite.
All inputs are finite; a program needn't handle non-finite values. No bound on the sum of `land_mask` on one device may be relied on, other than what follows from the above.
Results may differ from the reference program's by a relative error of at most 0.0003.
Values sent between devices are 32-bit elements; how exact they have to be, the bound alone decides.
A program may use at most 128 MiB of HBM per device.

```python
import math
import jax
import jax.numpy as jnp
from jax import lax

TR = 2
LEV = 40
CX = 8
CY = 128
SLOTS = 32
RB = 256
ITERS = 2
NX = 64
NY = 512
NODES = 32
NB = 4
CELLS_DEV = 81920
N_GX = 8
N_GY = 4


def draw_obs_count(key, part):
    first, second, third = jax.random.split(key, 3)
    base = jax.random.randint(first, (NODES, NODES), 0, SLOTS + 1)
    density = jax.random.randint(second, (1, NODES), 1, 5)
    full_owner = jax.random.randint(third, (), 0, NODES)
    counted = jnp.minimum(base * density // 2, SLOTS)
    owners = jnp.arange(NODES, dtype=jnp.int32)[None, :]
    return jnp.where(owners == full_owner, SLOTS, counted).astype(jnp.int32)


def draw_obs_weight(key, part):
    first, second = jax.random.split(key)
    spread = jnp.exp(jax.random.uniform(first, (NODES, NB, RB), jnp.float32, 0.0, math.log(3.0)))
    raw = jax.random.uniform(second, (NODES, NB, RB, RB), jnp.float32, -1.0, 1.0)
    symmetric = 0.5 * (raw + jnp.swapaxes(raw, 2, 3))
    identity = jnp.eye(RB, dtype=jnp.float32)
    inner_part = identity + 0.9 / (RB - 1) * symmetric * (1.0 - identity)
    return spread[:, :, :, None] * spread[:, :, None, :] * inner_part


def with_ends(drawn, rng, least, high):
    longest = drawn.shape.index(max(drawn.shape))
    spots = []
    for shift in (0, 1):
        where = [jax.random.randint(jax.random.fold_in(rng, axis), (), 0, length) for axis, length in enumerate(drawn.shape)]
        where[longest] = (where[longest] + shift) % drawn.shape[longest]
        spots.append(tuple(where))
    return drawn.at[spots[0]].set(least).at[spots[1]].set(high)


def block_levels(stream_key, extent, pieces, smallest, top_value):
    loudness, own = 1.0, jax.random.fold_in(stream_key, 6)
    for position, blocks in pieces:
        heights = jnp.exp(jax.random.uniform(jax.random.fold_in(own, position), (blocks,), jnp.float32, smallest / len(pieces), top_value / len(pieces)))
        loudness = loudness * jnp.repeat(heights, extent[position] // blocks).reshape([-1 if axis == position else 1 for axis in range(len(extent))])
    return loudness


def gaussian(own_key, shape, width, limit, shards=(), kind=jnp.bfloat16):
    array = width * jax.random.normal(own_key, shape, jnp.float32)
    if shards:
        array = array * block_levels(own_key, shape, shards, -0.22, 0.18)
    return jnp.clip(array, -limit, limit).astype(kind)


def setup_inputs(seed: int = 0) -> dict:
    seeds = jax.random.split(jax.random.key(seed), 8)
    return {
        "rate_x": jnp.clip(jnp.exp(math.log(0.25) - 4.6051702 * jax.random.uniform(seeds[0], (LEV, NX, NY), jnp.float32) ** block_levels(seeds[0], (LEV, NX, NY), ((1, 8), (2, 4)), -0.2, 0.2)), 0.0025, 0.25),
        "rate_y": jnp.clip(jnp.exp(math.log(0.015625) - 4.6051702 * jax.random.uniform(seeds[1], (LEV, NX, NY), jnp.float32) ** block_levels(seeds[1], (LEV, NX, NY), ((1, 8), (2, 4)), -0.2, 0.2)), 0.00015625, 0.015625),
        "land_mask": with_ends((jax.random.randint(seeds[2], (NX, NY), 0, 5) < 4).astype(jnp.int32), jax.random.fold_in(seeds[2], 1), 0, 1),
        "obs_cell": with_ends(jax.random.randint(seeds[3], (NODES, NODES, SLOTS), 0, CELLS_DEV), jax.random.fold_in(seeds[3], 1), 0, CELLS_DEV - 1).astype(jnp.int32),
        "obs_count": draw_obs_count(jax.random.fold_in(seeds[7], 71), 0),
        "innovation": gaussian(seeds[5], (NODES, NODES, SLOTS), 2.0, 12.0, ((0, 32),), jnp.float32),
        "obs_weight": draw_obs_weight(jax.random.fold_in(seeds[7], 71), 0),
    }


def compose_maps(earlier, following):
    return (earlier[0] * following[0], following[0] * earlier[1] + following[1])

def line_solve(state_field, decay_rate, line_axis, periodic):
    retention = jnp.broadcast_to(jnp.exp(-decay_rate), state_field.shape)
    one_minus = -jnp.expm1(-decay_rate)
    scaling = jnp.sqrt(one_minus * (1.0 + jnp.exp(-decay_rate)))
    weight = jnp.sqrt(jnp.sqrt(one_minus))
    line_length = state_field.shape[line_axis]
    factor, offset = lax.associative_scan(compose_maps, (retention, scaling * weight * state_field), axis=line_axis)
    if periodic:
        start_state = lax.index_in_dim(offset, line_length - 1, line_axis) / (1.0 - lax.index_in_dim(factor, line_length - 1, line_axis))
        forward = offset + factor * start_state
    else:
        forward = offset
    flipped = lax.associative_scan(compose_maps, (jnp.flip(retention, line_axis), jnp.flip(retention * forward, line_axis)), axis=line_axis)
    back_factor = jnp.flip(flipped[0], line_axis)
    back_offset = jnp.flip(flipped[1], line_axis)
    next_factor = jnp.concatenate([lax.slice_in_dim(back_factor, 1, line_length, axis=line_axis), jnp.ones_like(lax.slice_in_dim(back_factor, 0, 1, axis=line_axis))], axis=line_axis)
    next_offset = jnp.concatenate([lax.slice_in_dim(back_offset, 1, line_length, axis=line_axis), jnp.zeros_like(lax.slice_in_dim(back_offset, 0, 1, axis=line_axis))], axis=line_axis)
    if periodic:
        entering = lax.index_in_dim(back_offset, 0, line_axis) / (1.0 - lax.index_in_dim(back_factor, 0, line_axis))
        later_part = next_offset + next_factor * entering
    else:
        later_part = next_offset
    return weight * scaling * (forward + later_part)

def to_blocks(state_field):
    shaped = state_field.reshape(TR, LEV, N_GX, CX, N_GY, CY).transpose(2, 4, 0, 1, 3, 5)
    return shaped.reshape(NODES, CELLS_DEV)

def from_blocks(owned):
    shaped = owned.reshape(N_GX, N_GY, TR, LEV, CX, CY).transpose(2, 3, 0, 4, 1, 5)
    return shaped.reshape(TR, LEV, NX, NY)

def reference(rate_x, rate_y, land_mask, obs_cell, obs_count, innovation, obs_weight):
    ocean = land_mask.astype(jnp.float32)

    def spread(vector):
        return ocean * line_solve(line_solve(ocean * vector, rate_x, 2, True), rate_y, 3, False)

    def gather_back(vector):
        return ocean * line_solve(line_solve(ocean * vector, rate_y, 3, False), rate_x, 2, True)
    occupied = (jnp.arange(SLOTS, dtype=jnp.int32)[None, None, :] < obs_count[:, :, None]).astype(jnp.float32)
    cell_index = obs_cell.reshape(NODES, NODES * SLOTS).astype(jnp.int32)

    def weigh_obs(values):
        packed = (occupied * values).reshape(NODES, NB, RB)
        mixed = jnp.einsum('snij,snj->sni', obs_weight, packed, precision=lax.Precision.HIGHEST)
        return occupied * mixed.reshape(NODES, NODES, SLOTS)

    def observe(vector):
        picked = jnp.take_along_axis(to_blocks(vector), cell_index, axis=1).reshape(NODES, NODES, SLOTS)
        return jnp.transpose(picked, (1, 0, 2))

    def deposit(values):
        owner_view = jnp.transpose(values, (1, 0, 2)).reshape(NODES, NODES * SLOTS)

        def add_block(positions, amounts):
            return jnp.zeros((CELLS_DEV,), jnp.float32).at[positions].add(amounts)
        return from_blocks(jax.vmap(add_block)(cell_index, owner_view))
    right_side = gather_back(deposit(weigh_obs(innovation)))
    solution = jnp.zeros_like(right_side)
    residual = right_side
    direction = right_side
    norm_now = jnp.sum(residual * residual)
    for iteration in range(ITERS):
        hessian_dir = direction + gather_back(deposit(weigh_obs(observe(spread(direction)))))
        step_length = norm_now / jnp.sum(direction * hessian_dir)
        solution = solution + step_length * direction
        residual = residual - step_length * hessian_dir
        norm_next = jnp.sum(residual * residual)
        direction = residual + norm_next / norm_now * direction
        norm_now = norm_next
    return (solution, residual)
```

```python
import functools

import jax
import jax.numpy as jnp
from jax import lax
from jax.experimental import pallas as pl
from jax.experimental.pallas import tpu as pltpu
from jax.sharding import PartitionSpec as P

TR = 2
ITERS = 2
SUB = 8
LANE = 128
GL = 8
MESH = pl.DeviceIdType.MESH
F32 = jnp.float32
BF16 = jnp.bfloat16


def split3(a):
    hi = a.astype(BF16)
    rest = a - hi.astype(F32)
    mid = rest.astype(BF16)
    lo = (rest - mid.astype(F32)).astype(BF16)
    return hi, mid, lo


def kernel(
    nx, ny, lev, slots,
    dx, wx, dy, wy, ocean_ref, cell, occ, innov, wobs,
    sol, res,
    drn, v, ob, qb, fld, ffx, fbx, k1x, k2x, ffy, fby, k1y, k2y,
    ex, xx, rows1h, lanes1h, yold, xinv, xown,
    as_, ar, xs1, xr1, xs2, xr2, ys, yr,
    a_ss, a_rs, x1_ss, x1_rs, x2_ss, x2_rs, y_ss, y_rs,
):
    nodes = nx * ny
    per = LANE // slots
    nch = nodes * slots // LANE
    rr_rows = TR * lev // nx
    R = rr_rows
    G = lev // GL
    mx = lax.axis_index("gx")
    my = lax.axis_index("gy")
    me = mx * ny + my
    NXP = 2 * ITERS + 1

    barrier = pltpu.get_barrier_semaphore()

    def greet(off, c):
        d = lax.rem(me + off, nodes)
        pl.semaphore_signal(barrier, inc=1, device_id=(d // ny, lax.rem(d, ny)), device_id_type=MESH)
        return c

    lax.fori_loop(1, nodes, greet, 0)

    sub_i = lax.broadcasted_iota(jnp.int32, (GL, SUB, LANE), 1)
    lane_i = lax.broadcasted_iota(jnp.int32, (GL, SUB, LANE), 2)
    four = (TR, GL, SUB, LANE)
    tag = (
        lax.broadcasted_iota(jnp.int32, four, 3)
        - lax.broadcasted_iota(jnp.int32, four, 0) * lev
        - lax.broadcasted_iota(jnp.int32, four, 1)
    )
    ocean = ocean_ref[...]

    def steps(n):
        out, s = [], 1
        while s < n:
            out.append(s)
            s *= 2
        return out

    def scan(a, fac, lv, n, axis, back, g):
        for k, s in enumerate(steps(n)):
            a = a + fac[k, pl.ds(GL * g, GL)] * pltpu.roll(a, (n - s) if back else s, axis)
        return a

    def coefficients(d_ref, w_ref, ff, fb, k1, k2, n, ax, g):
        at = pl.ds(GL * g, GL)
        i = sub_i if ax == 1 else lane_i
        d = d_ref[at]
        w = w_ref[at]
        p = d
        b = d
        for k, s in enumerate(steps(n)):
            ff[k, at] = jnp.where(i >= s, p, 0.0)
            p = p * jnp.where(i >= s, pltpu.roll(p, s, ax), 1.0)
            fb[k, at] = jnp.where(i < n - s, b, 0.0)
            b = b * jnp.where(i < n - s, pltpu.roll(b, n - s, ax), 1.0)
        c = scan(d * p, fb, None, n, ax, True, g)
        k1[at] = w * (p + jnp.where(i < n - 1, pltpu.roll(c, n - 1, ax), 0.0))
        k2[at] = w * jnp.where(i < n - 1, pltpu.roll(b, n - 1, ax), 1.0)
        return p, c

    def put_rows(ref, a, g):
        for t in range(TR):
            start = pl.multiple_of((t * lev + GL * g) * SUB, GL * SUB)
            ref[pl.ds(start, GL * SUB), :] = a[t].reshape(GL * SUB, LANE)

    def local_x(u, g):
        at = pl.ds(GL * g, GL)
        w = wx[at]
        o = scan(w * u, ffx, None, SUB, 2, False, g)
        q = scan(dx[at] * o, fbx, None, SUB, 2, True, g)
        v[:, at] = w * (o + jnp.where(sub_i < SUB - 1, pltpu.roll(q, SUB - 1, 2), 0.0))
        put_rows(ob, o, g)
        put_rows(qb, q, g)

    def pick(a, col, g):
        column = jnp.broadcast_to(a[..., col : col + 1], four)
        return jnp.sum(jnp.where(tag == GL * g, column, 0.0), axis=(0, 1))

    def local_y(u, g):
        at = pl.ds(GL * g, GL)
        w = wy[at]
        o = scan(w * u, ffy, None, LANE, 3, False, g)
        q = scan(dy[at] * o, fby, None, LANE, 3, True, g)
        v[:, at] = w * (o + jnp.where(lane_i < LANE - 1, pltpu.roll(q, LANE - 1, 3), 0.0))
        return pick(o, LANE - 1, g), pick(q, 0, g)

    def after_x(g):
        at = pl.ds(GL * g, GL)

        def rows(ref):
            parts = [ref[pl.ds(pl.multiple_of(t * lev + GL * g, GL), GL), :] for t in range(TR)]
            return jnp.stack([p.reshape(GL, 1, LANE) for p in parts])

        return v[:, at] + k1x[at] * rows(ex) + k2x[at] * rows(xx)

    def after_y(e, x, g):
        at = pl.ds(GL * g, GL)

        def column(a):
            return jnp.sum(jnp.where(tag == GL * g, a, 0.0), axis=3, keepdims=True)

        return v[:, at] + k1y[at] * column(e) + k2y[at] * column(x)

    zero = jnp.zeros((SUB, LANE), F32)

    def wait_all(buf, sem):
        pltpu.make_async_copy(buf, buf, sem).wait()

    def x_start(src, dst, ss, rs, p):
        def one(off, c):
            j = lax.rem(mx + off, nx)
            pltpu.make_async_remote_copy(
                src_ref=src.at[p, j], dst_ref=dst.at[p, mx], send_sem=ss.at[p], recv_sem=rs.at[p],
                device_id=(j, my), device_id_type=MESH,
            ).start()
            return c

        lax.fori_loop(1, nx, one, 0)
        dst[p, mx] = src[p, mx]

    def x_wait(src, dst, ss, rs, p):
        wait_all(dst.at[p, pl.ds(0, nx - 1)], rs.at[p])
        wait_all(src.at[p, pl.ds(0, nx - 1)], ss.at[p])

    def x_fill(p, row):
        for j in range(nx):
            xs1[p, j, 0:R] = ob[pl.ds(SUB - 1 + SUB * R * j, R, stride=SUB), :]
            xs1[p, j, R : 2 * R] = qb[pl.ds(SUB * R * j, R, stride=SUB), :]
            xs1[p, j, 2 * R : 2 * R + 1] = row

    def x_exchange(p, row):
        x_fill(p, row)
        x_start(xs1, xr1, x1_ss, x1_rs, p)
        x_wait(xs1, xr1, x1_ss, x1_rs, p)
        A = [xown[j, 0:R] for j in range(nx)]
        C = [xown[j, R : 2 * R] for j in range(nx)]
        F = [xr1[p, j, 0:R] for j in range(nx)]
        B = [xr1[p, j, R : 2 * R] for j in range(nx)]
        inv = xinv[0:R]
        e = F[0]
        for j in range(1, nx):
            e = F[j] + A[j] * e
        e = e * inv
        gs = []
        for j in range(nx):
            xs2[p, j, 0:R] = e
            gs.append(B[j] + C[j] * e)
            e = F[j] + A[j] * e
        x = gs[nx - 1]
        for j in range(nx - 2, -1, -1):
            x = gs[j] + A[j] * x
        x = x * inv
        for j in range(nx - 1, -1, -1):
            xs2[p, j, R : 2 * R] = x
            x = gs[j] + A[j] * x
        x_start(xs2, xr2, x2_ss, x2_rs, p)
        total = xr1[p, 0, 2 * R : 2 * R + 1]
        for j in range(1, nx):
            total = total + xr1[p, j, 2 * R : 2 * R + 1]
        x_wait(xs2, xr2, x2_ss, x2_rs, p)
        for j in range(nx):
            ex[R * j : R * (j + 1)] = xr2[p, j, 0:R]
            xx[R * j : R * (j + 1)] = xr2[p, j, R : 2 * R]
        return total

    def y_start(p, f, b, row):
        ys[p, 0:SUB] = f
        ys[p, SUB : 2 * SUB] = b
        ys[p, 2 * SUB : 3 * SUB] = jnp.broadcast_to(row, (SUB, LANE))

        def one(off, c):
            j = lax.rem(my + off, ny)
            pltpu.make_async_remote_copy(
                src_ref=ys.at[p], dst_ref=yr.at[p, my], send_sem=y_ss.at[p], recv_sem=y_rs.at[p],
                device_id=(mx, j), device_id_type=MESH,
            ).start()
            return c

        lax.fori_loop(1, ny, one, 0)
        yr[p, my] = ys[p]

    def y_wait(p):
        wait_all(yr.at[p, pl.ds(0, ny - 1)], y_rs.at[p])
        wait_all(yr.at[p, pl.ds(0, ny - 1)], y_ss.at[p])

    def y_exchange(p, f, b, row):
        y_start(p, f, b, row)
        y_wait(p)
        total = yr[p, 0, 2 * SUB : 2 * SUB + 1]
        for j in range(1, ny):
            total = total + yr[p, j, 2 * SUB : 2 * SUB + 1]
        e, mine_e, gs = zero, zero, []
        for j in range(ny):
            mine_e = jnp.where(my == j, e, mine_e)
            gs.append(yr[p, j, SUB : 2 * SUB] + yr[NXP, j, SUB : 2 * SUB] * e)
            e = yr[p, j, 0:SUB] + yr[NXP, j, 0:SUB] * e
        x, mine_x = zero, zero
        for j in range(ny - 1, -1, -1):
            mine_x = jnp.where(my == j, x, mine_x)
            x = gs[j] + yr[NXP, j, 0:SUB] * x
        return mine_e, mine_x, total

    def a_start(p, chunks):
        for c in range(nch):
            as_[p, c] = chunks[c]

        def one(off, c):
            d = lax.rem(me + off, nodes)
            pltpu.make_async_remote_copy(
                src_ref=as_.at[p, d // per], dst_ref=ar.at[p, me], send_sem=a_ss.at[p], recv_sem=a_rs.at[p],
                device_id=(d // ny, lax.rem(d, ny)), device_id_type=MESH,
            ).start()
            return c

        lax.fori_loop(1, nodes, one, 0)
        ar[p, me] = as_[p, me // per]

    def a_wait(p):
        wait_all(ar.at[p, pl.ds(0, nodes - 1)], a_rs.at[p])
        wait_all(ar.at[p, pl.ds(0, nodes - 1)], a_ss.at[p])
        got = ar[p].reshape(nch, per, 1, LANE)
        block = lax.broadcasted_iota(jnp.int32, (nch, 1, LANE), 2) // slots
        mine = lax.rem(me, per)
        total = jnp.zeros((nch, 1, LANE), F32)
        for i in range(per):
            turned = pltpu.roll(got[:, i], lax.rem(i - mine + per, per) * slots, 2)
            total = jnp.where(block == i, turned, total)
        return total

    def weigh(y):
        y = occ[...] * y
        per_block = wobs.shape[1] // LANE
        chunks = []
        for n in range(wobs.shape[0]):
            row = jnp.concatenate([y[per_block * n + a] for a in range(per_block)], axis=1)
            z = lax.dot_general(
                jnp.broadcast_to(row, (SUB, row.shape[1])), wobs[n], (((1,), (1,)), ((), ())),
                precision=lax.Precision.HIGHEST, preferred_element_type=F32,
            )
            for a in range(per_block):
                chunks.append(z[0:1, a * LANE : (a + 1) * LANE] * occ[per_block * n + a])
        return chunks

    def onehots():
        ri = lax.broadcasted_iota(jnp.int32, (TR * lev * SUB, LANE), 0)
        li = lax.broadcasted_iota(jnp.int32, (LANE, LANE), 0)
        for c in range(nch):
            here = cell[c]
            cols = slice(c * LANE, (c + 1) * LANE)
            rows1h[:, cols] = jnp.where(ri == here // LANE, 1.0, 0.0).astype(BF16)
            lanes1h[:, cols] = jnp.where(li == lax.rem(here, LANE), 1.0, 0.0)

    def observe():
        t = jnp.transpose(fld[...].reshape(TR * lev * SUB, LANE))
        lhs = jnp.concatenate(split3(t), axis=0)
        chunks = []
        for c in range(nch):
            cols = slice(c * LANE, (c + 1) * LANE)
            got = jnp.dot(lhs, rows1h[:, cols], preferred_element_type=F32)
            got = (got[0:LANE] + got[LANE : 2 * LANE]) + got[2 * LANE :]
            chunks.append(jnp.sum(got * lanes1h[:, cols], axis=0, keepdims=True))
        return chunks

    def deposit(vals):
        row = jnp.concatenate([vals[c] for c in range(nch)], axis=1)
        rhs = jnp.concatenate(split3(lanes1h[...] * row), axis=0)
        got = lax.dot_general(rows1h[...], rhs, (((1,), (1,)), ((), ())), preferred_element_type=F32)
        got = (got[:, 0:LANE] + got[:, LANE : 2 * LANE]) + got[:, 2 * LANE :]
        fld[...] = got.reshape(TR, lev, SUB, LANE)

    def lane_total(row):
        return jnp.broadcast_to(jnp.sum(row, axis=1, keepdims=True), (1, LANE))

    def fold(tile):
        return jnp.sum(tile, axis=0, keepdims=True)

    def forth(p, row, body):
        vals = a_wait(p)
        deposit(vals)

        def first(g, c):
            f, b = local_y(ocean * fld[:, pl.ds(GL * g, GL)], g)
            return c[0] + f, c[1] + b

        f, b = lax.fori_loop(0, G, first, (zero, zero))
        e, x, total = y_exchange(p, f, b, row)

        def second(g, c):
            local_x(after_y(e, x, g), g)
            return c

        lax.fori_loop(0, G, second, 0)
        total = lane_total(x_exchange(p, total))
        return fold(lax.fori_loop(0, G, lambda g, c: body(g, c, ocean * after_x(g), total), zero))

    def back(p, row, body):
        def first(g, c):
            local_x(ocean * res[:, pl.ds(GL * g, GL)], g)
            return c

        lax.fori_loop(0, G, first, 0)
        total = x_exchange(p, row)

        def second(g, c):
            f, b = local_y(after_x(g), g)
            return c[0] + f, c[1] + b

        f, b = lax.fori_loop(0, G, second, (zero, zero))
        e, x, total = y_exchange(p, f, b, total)
        total = lane_total(total)

        def third(g, c):
            fld[:, pl.ds(GL * g, GL)] = ocean * after_y(e, x, g)
            return body(g, c, total)

        dd = fold(lax.fori_loop(0, G, third, zero))
        a_start(p, observe())
        return a_wait(p), dd, total

    for buf in (xs1, xs2):
        buf[...] = jnp.zeros(buf.shape, F32)
    chunks = weigh(innov[...])
    pl.semaphore_wait(barrier, nodes - 1)
    a_start(0, chunks)

    def prepare(g, c):
        p, b = coefficients(dx, wx, ffx, fbx, k1x, k2x, SUB, 1, g)
        put_rows(ob, [p] * TR, g)
        put_rows(qb, [b] * TR, g)
        p, b = coefficients(dy, wy, ffy, fby, k1y, k2y, LANE, 2, g)
        p = jnp.broadcast_to(p[None], four)
        b = jnp.broadcast_to(b[None], four)
        return c[0] + pick(p, LANE - 1, g), c[1] + pick(b, 0, g)

    a, c = lax.fori_loop(0, G, prepare, (zero, zero))
    y_start(NXP, a, c, zero[0:1])
    x_fill(NXP, zero[0:1])
    x_start(xs1, xr1, x1_ss, x1_rs, NXP)
    onehots()
    y_wait(NXP)
    x_wait(xs1, xr1, x1_ss, x1_rs, NXP)
    xown[...] = xr1[NXP]
    whole = xown[0, 0:R]
    for j in range(1, nx):
        whole = whole * xown[j, 0:R]
    xinv[0:R] = 1.0 / (1.0 - whole)

    def begin(g, c, image, total):
        at = pl.ds(GL * g, GL)
        res[:, at] = image
        drn[:, at] = jnp.zeros(four, F32)
        sol[:, at] = jnp.zeros(four, F32)
        return c + jnp.sum(image * image, axis=(0, 1))

    rr_part = forth(0, zero[0:1], begin)
    rr_old = None
    for it in range(ITERS):
        beta_of = (lambda t: jnp.zeros_like(t)) if it == 0 else (lambda t, o=rr_old: t / o)

        def turn(g, c, total):
            at = pl.ds(GL * g, GL)
            new = res[:, at] + beta_of(total) * drn[:, at]
            drn[:, at] = new
            return c + jnp.sum(new * new, axis=(0, 1))

        y, dd, rr = back(2 * it + 1, rr_part, turn)
        if it > 0:
            y = y + beta_of(rr) * yold[...]
        yold[...] = y
        chunks = weigh(y)
        a_start(2 * it + 2, chunks)
        for k in range(nch):
            dd = dd + y[k] * chunks[k]

        def update(g, c, term, total):
            at = pl.ds(GL * g, GL)
            alpha = rr / total
            d = drn[:, at]
            sol[:, at] = sol[:, at] + alpha * d
            new = res[:, at] - alpha * (d + term)
            res[:, at] = new
            return c + jnp.sum(new * new, axis=(0, 1))

        rr_part = forth(2 * it + 2, dd, update)
        rr_old = rr


def on_device(nx, ny, rate_x, rate_y, land_mask, obs_cell, obs_count, innovation, obs_weight):
    lev, cx, cy = rate_x.shape
    slots = obs_cell.shape[2]
    nodes = nx * ny
    nch = nodes * slots // LANE
    assert (cx, cy) == (SUB, LANE) and lev % GL == 0 and (TR * lev) % nx == 0
    assert TR * lev <= LANE and LANE % slots == 0

    def plan(rate):
        decay = jnp.exp(-rate)
        one_minus = -jnp.expm1(-rate)
        scaling = jnp.sqrt(one_minus * (1.0 + decay))
        return decay, scaling * jnp.sqrt(jnp.sqrt(one_minus))

    dx, wx = plan(rate_x)
    dy, wy = plan(rate_y)
    occupied = (
        lax.broadcasted_iota(jnp.int32, (nodes, slots), 1) < obs_count[0][:, None]
    ).astype(F32)
    R = TR * lev // nx
    M = (2 * R + 1 + 7) // 8 * 8
    NXP = 2 * ITERS + 1
    field = (TR, lev, SUB, LANE)
    one = (lev, SUB, LANE)
    vm = pltpu.VMEM
    dma = pltpu.SemaphoreType.DMA
    Rp = (R + 7) // 8 * 8
    return pl.pallas_call(
        functools.partial(kernel, nx, ny, lev, slots),
        out_shape=(jax.ShapeDtypeStruct(field, F32),) * 2,
        in_specs=[pl.BlockSpec(memory_space=vm)] * 9,
        out_specs=(pl.BlockSpec(memory_space=vm),) * 2,
        scratch_shapes=[
            vm(field, F32), vm(field, F32),
            vm((TR * lev * SUB, LANE), F32), vm((TR * lev * SUB, LANE), F32),
            vm(field, F32),
            vm((3,) + one, F32), vm((3,) + one, F32), vm(one, F32), vm(one, F32),
            vm((7,) + one, F32), vm((7,) + one, F32), vm(one, F32), vm(one, F32),
            vm((TR * lev, LANE), F32), vm((TR * lev, LANE), F32),
            vm((TR * lev * SUB, nch * LANE), BF16), vm((LANE, nch * LANE), F32),
            vm((nch, 1, LANE), F32), vm((Rp, LANE), F32), vm((nx, M, LANE), F32),
            vm((NXP, nch, 1, LANE), F32), vm((NXP, nodes, 1, LANE), F32),
            vm((NXP + 1, nx, M, LANE), F32), vm((NXP + 1, nx, M, LANE), F32),
            vm((NXP, nx, M, LANE), F32), vm((NXP, nx, M, LANE), F32),
            vm((NXP + 1, 3 * SUB, LANE), F32), vm((NXP + 1, ny, 3 * SUB, LANE), F32),
            dma((NXP,)), dma((NXP,)), dma((NXP + 1,)), dma((NXP + 1,)),
            dma((NXP,)), dma((NXP,)), dma((NXP + 1,)), dma((NXP + 1,)),
        ],
        compiler_params=pltpu.CompilerParams(
            collective_id=0, has_side_effects=True, vmem_limit_bytes=56 * 1024 * 1024
        ),
    )(
        dx, wx, dy, wy, land_mask.astype(F32),
        obs_cell.reshape(nch, 1, LANE), occupied.reshape(nch, 1, LANE),
        innovation.reshape(nch, 1, LANE), obs_weight[0],
    )


def solution(mesh):
    placed = (
        P(None, "gx", "gy"),
        P(None, "gx", "gy"),
        P("gx", "gy"),
        P(("gx", "gy"), None, None),
        P(("gx", "gy"), None),
        P(("gx", "gy"), None, None),
        P(("gx", "gy"), None, None, None),
    )
    return jax.shard_map(
        functools.partial(on_device, mesh.shape["gx"], mesh.shape["gy"]),
        mesh=mesh,
        in_specs=placed,
        out_specs=(P(None, None, "gx", "gy"), P(None, None, "gx", "gy")),
        check_vma=False,
    )
```

```python
import functools

import jax
import jax.numpy as jnp
from jax import lax
from jax.experimental import pallas as pl
from jax.experimental.pallas import tpu as pltpu
from jax.sharding import PartitionSpec as P

TR = 2
ITERS = 2
SUB = 8
LANE = 128
MESH = pl.DeviceIdType.MESH
F32 = jnp.float32
BF16 = jnp.bfloat16


def split3(a):
    hi = a.astype(BF16)
    rest = a - hi.astype(F32)
    mid = rest.astype(BF16)
    lo = (rest - mid.astype(F32)).astype(BF16)
    return hi, mid, lo


def kernel(
    nx, ny, lev, slots,
    rx, ry, mask_ref, cell, count, innov, wobs,
    sol, res,
    drn, v, ob, qb, cx, cy, tri,
    ex, xx, rows1h, lanes1h, occ, yold, xinv, xown,
    as_, ar, xs1, xr1, xs2, xr2, ys, yr,
    a_ss, a_rs, x1_ss, x1_rs, x2_ss, x2_rs, y_ss, y_rs,
):
    nodes = nx * ny
    per = LANE // slots
    nch = nodes * slots // LANE
    lines = TR * lev
    R = lines // nx
    mx = lax.axis_index("gx")
    my = lax.axis_index("gy")
    me = mx * ny + my
    NXP = 2 * ITERS + 1
    gxs = [lax.rem(mx + j, nx) for j in range(nx)]
    gys = [lax.rem(my + j, ny) for j in range(ny)]
    others = [(i, j) for i in range(nx) for j in range(ny) if i or j]

    barrier = pltpu.get_barrier_semaphore()
    for i, j in others:
        pl.semaphore_signal(barrier, inc=1, device_id=(gxs[i], gys[j]), device_id_type=MESH)

    one = (lev, SUB, LANE)
    four = (TR, lev, SUB, LANE)
    sub_i = lax.broadcasted_iota(jnp.int32, (SUB, LANE), 0)
    lane_i = lax.broadcasted_iota(jnp.int32, (SUB, LANE), 1)
    ocean = mask_ref[...].astype(F32)

    def sums_x(a, back):
        ax = a.ndim - 2
        for s in (1, 2, 4):
            if back:
                a = a + jnp.where(sub_i < SUB - s, pltpu.roll(a, SUB - s, ax), 0.0)
            else:
                a = a + jnp.where(sub_i >= s, pltpu.roll(a, s, ax), 0.0)
        return a

    def sums_x_after(a):
        b = sums_x(a, True)
        return b, jnp.where(sub_i < SUB - 1, pltpu.roll(b, SUB - 1, a.ndim - 2), 0.0)

    def sums_y(a, which):
        flat = a.reshape(a.size // LANE, LANE)
        lhs = jnp.concatenate(split3(flat), axis=1)
        return jnp.dot(lhs, tri[which], preferred_element_type=F32).reshape(a.shape)

    def shape_of(rate):
        decay = jnp.exp(-rate)
        series = 1.0
        for k in (9, 8, 7, 6, 5, 4, 3, 2):
            series = 1.0 - series * rate * (1.0 / k)
        one_minus = rate * series
        return jnp.sqrt(one_minus * (1.0 + decay)) * jnp.sqrt(jnp.sqrt(one_minus))

    def coefficients(co, w, c, end, after):
        p = jnp.exp(-c)
        pinv = jnp.exp(c)
        p2 = p * p
        total, later = after(p2)
        co[0] = w * pinv
        co[1] = p
        co[2] = w * p
        co[3] = p2
        co[4] = w * (p + pinv * later)
        co[5] = w * jnp.exp(c - end)
        return p, total

    def put_rows(ref, a):
        ref[...] = a.reshape(lines * SUB, LANE)

    def local_x(u):
        s = sums_x(u * cx[0], False)
        total, later = sums_x_after(s * cx[3])
        v[...] = cx[2] * s + cx[0] * later
        put_rows(ob, cx[1] * s)
        put_rows(qb, total)

    tag = (
        lax.broadcasted_iota(jnp.int32, four, 3)
        - lax.broadcasted_iota(jnp.int32, four, 0) * lev
        - lax.broadcasted_iota(jnp.int32, four, 1)
    )

    def pick(a, col):
        column = jnp.broadcast_to(a[..., col : col + 1], four)
        return jnp.sum(jnp.where(tag == 0, column, 0.0), axis=(0, 1))

    def local_y(u):
        s = sums_y(u * cy[0], 0)
        m = s * cy[3]
        later = sums_y(m, 1)
        v[...] = cy[2] * s + cy[0] * later
        return pick(cy[1] * s, LANE - 1), pick(later + m, 0)

    def after_x():
        def rows(ref):
            return ref[...].reshape(TR, lev, 1, LANE)

        return v[...] + cx[4] * rows(ex) + cx[5] * rows(xx)

    def after_y(e, x):
        def columns(a):
            parts = [jnp.broadcast_to(a[:, t : t + 1], (SUB, LANE)) for t in range(lines)]
            return jnp.stack(parts).reshape(four)

        return v[...] + cy[4] * columns(e) + cy[5] * columns(x)

    zero = jnp.zeros((SUB, LANE), F32)
    zero_row = jnp.zeros((1, LANE), F32)

    def wait_all(buf, sem):
        pltpu.make_async_copy(buf, buf, sem).wait()

    def x_start(src, dst, ss, rs, p):
        for i in range(1, nx):
            pltpu.make_async_remote_copy(
                src_ref=src.at[p, gxs[i]], dst_ref=dst.at[p, mx], send_sem=ss.at[p], recv_sem=rs.at[p],
                device_id=(gxs[i], my), device_id_type=MESH,
            ).start()
        dst[p, mx] = src[p, mx]

    def x_wait(src, dst, ss, rs, p):
        wait_all(dst.at[p, pl.ds(0, nx - 1)], rs.at[p])
        wait_all(src.at[p, pl.ds(0, nx - 1)], ss.at[p])

    def x_fill(p, row):
        for j in range(nx):
            xs1[p, j, 0:R] = ob[pl.ds(SUB - 1 + SUB * R * j, R, stride=SUB), :]
            xs1[p, j, R : 2 * R] = qb[pl.ds(SUB * R * j, R, stride=SUB), :]
            xs1[p, j, 2 * R : 2 * R + 1] = row

    def x_exchange(p, row):
        x_fill(p, row)
        x_start(xs1, xr1, x1_ss, x1_rs, p)
        x_wait(xs1, xr1, x1_ss, x1_rs, p)
        A = [xown[j, 0:R] for j in range(nx)]
        C = [xown[j, R : 2 * R] for j in range(nx)]
        F = [xr1[p, j, 0:R] for j in range(nx)]
        B = [xr1[p, j, R : 2 * R] for j in range(nx)]
        inv = xinv[0:R]
        e = F[0]
        for j in range(1, nx):
            e = F[j] + A[j] * e
        e = e * inv
        gs = []
        for j in range(nx):
            xs2[p, j, 0:R] = e
            gs.append(B[j] + C[j] * e)
            e = F[j] + A[j] * e
        x = gs[nx - 1]
        for j in range(nx - 2, -1, -1):
            x = gs[j] + A[j] * x
        x = x * inv
        for j in range(nx - 1, -1, -1):
            xs2[p, j, R : 2 * R] = x
            x = gs[j] + A[j] * x
        x_start(xs2, xr2, x2_ss, x2_rs, p)
        total = xr1[p, 0, 2 * R : 2 * R + 1]
        for j in range(1, nx):
            total = total + xr1[p, j, 2 * R : 2 * R + 1]
        x_wait(xs2, xr2, x2_ss, x2_rs, p)
        for j in range(nx):
            ex[R * j : R * (j + 1)] = xr2[p, j, 0:R]
            xx[R * j : R * (j + 1)] = xr2[p, j, R : 2 * R]
        return total

    def y_start(p, f, b, row):
        ys[p, 0:SUB] = f
        ys[p, SUB : 2 * SUB] = b
        ys[p, 2 * SUB : 3 * SUB] = jnp.broadcast_to(row, (SUB, LANE))
        for j in range(1, ny):
            pltpu.make_async_remote_copy(
                src_ref=ys.at[p], dst_ref=yr.at[p, my], send_sem=y_ss.at[p], recv_sem=y_rs.at[p],
                device_id=(mx, gys[j]), device_id_type=MESH,
            ).start()
        yr[p, my] = ys[p]

    def y_wait(p):
        wait_all(yr.at[p, pl.ds(0, ny - 1)], y_rs.at[p])
        wait_all(yr.at[p, pl.ds(0, ny - 1)], y_ss.at[p])

    def y_exchange(p, f, b, row):
        y_start(p, f, b, row)
        y_wait(p)
        total = yr[p, 0, 2 * SUB : 2 * SUB + 1]
        for j in range(1, ny):
            total = total + yr[p, j, 2 * SUB : 2 * SUB + 1]
        e, mine_e, gs = zero, zero, []
        for j in range(ny):
            mine_e = jnp.where(my == j, e, mine_e)
            gs.append(yr[p, j, SUB : 2 * SUB] + yr[NXP, j, SUB : 2 * SUB] * e)
            e = yr[p, j, 0:SUB] + yr[NXP, j, 0:SUB] * e
        x, mine_x = zero, zero
        for j in range(ny - 1, -1, -1):
            mine_x = jnp.where(my == j, x, mine_x)
            x = gs[j] + yr[NXP, j, 0:SUB] * x
        return mine_e, mine_x, total

    def a_start(p, chunks):
        for c in range(nch):
            as_[p, c] = chunks[c]
        for i, j in others:
            pltpu.make_async_remote_copy(
                src_ref=as_.at[p, (gxs[i] * ny + gys[j]) // per], dst_ref=ar.at[p, me],
                send_sem=a_ss.at[p], recv_sem=a_rs.at[p],
                device_id=(gxs[i], gys[j]), device_id_type=MESH,
            ).start()
        ar[p, me] = as_[p, me // per]

    def a_wait(p):
        wait_all(ar.at[p, pl.ds(0, nodes - 1)], a_rs.at[p])
        wait_all(ar.at[p, pl.ds(0, nodes - 1)], a_ss.at[p])
        got = ar[p].reshape(nch, per, 1, LANE)
        block = lax.broadcasted_iota(jnp.int32, (nch, 1, LANE), 2) // slots
        mine = lax.rem(me, per)
        total = jnp.zeros((nch, 1, LANE), F32)
        for i in range(per):
            turned = pltpu.roll(got[:, i], lax.rem(i - mine + per, per) * slots, 2)
            total = jnp.where(block == i, turned, total)
        return total

    def line_up(ref, c):
        return jnp.concatenate([ref[0, per * c + i : per * c + i + 1, :] for i in range(per)], axis=1)

    def weigh(y):
        per_block = wobs.shape[2] // LANE
        chunks = []
        for n in range(wobs.shape[1]):
            row = jnp.concatenate([y[per_block * n + a] * occ[per_block * n + a] for a in range(per_block)], axis=1)
            z = lax.dot_general(
                jnp.broadcast_to(row, (SUB, row.shape[1])), wobs[0, n], (((1,), (1,)), ((), ())),
                precision=lax.Precision.HIGHEST, preferred_element_type=F32,
            )
            for a in range(per_block):
                chunks.append(z[0:1, a * LANE : (a + 1) * LANE] * occ[per_block * n + a])
        return chunks

    def onehots():
        ri = lax.broadcasted_iota(jnp.int32, (lines * SUB, LANE), 0)
        li = lax.broadcasted_iota(jnp.int32, (LANE, LANE), 0)
        for c in range(nch):
            here = line_up(cell, c)
            cols = slice(c * LANE, (c + 1) * LANE)
            rows1h[:, cols] = jnp.where(ri == here // LANE, 1.0, 0.0).astype(BF16)
            lanes1h[:, cols] = jnp.where(li == lax.rem(here, LANE), 1.0, 0.0)

    def observe(field):
        t = jnp.transpose(field.reshape(lines * SUB, LANE))
        lhs = jnp.concatenate(split3(t), axis=0)
        chunks = []
        for c in range(0, nch, 2):
            wide = min(2, nch - c)
            cols = slice(c * LANE, (c + wide) * LANE)
            got = jnp.dot(lhs, rows1h[:, cols], preferred_element_type=F32)
            got = (got[0:LANE] + got[LANE : 2 * LANE]) + got[2 * LANE :]
            got = jnp.sum(got * lanes1h[:, cols], axis=0, keepdims=True)
            chunks += [got[:, k * LANE : (k + 1) * LANE] for k in range(wide)]
        return chunks

    def deposit(vals):
        row = jnp.concatenate([vals[c] for c in range(nch)], axis=1)
        spread = lanes1h[...]
        rhs = jnp.concatenate([(spread * part.astype(F32)).astype(BF16) for part in split3(row)], axis=0)
        got = lax.dot_general(rows1h[...], rhs, (((1,), (1,)), ((), ())), preferred_element_type=F32)
        got = (got[:, 0:LANE] + got[:, LANE : 2 * LANE]) + got[:, 2 * LANE :]
        return got.reshape(four)

    def lane_total(row):
        return jnp.broadcast_to(jnp.sum(row, axis=1, keepdims=True), (1, LANE))

    def inner(a, b):
        return jnp.sum(jnp.sum(a * b, axis=(0, 1)), axis=0, keepdims=True)

    def forth(p, row):
        f, b = local_y(ocean * deposit(a_wait(p)))
        e, x, total = y_exchange(p, f, b, row)
        local_x(after_y(e, x))
        total = lane_total(x_exchange(p, total))
        return ocean * after_x(), total

    def back(p, row):
        local_x(ocean * res[...])
        total = x_exchange(p, row)
        f, b = local_y(after_x())
        e, x, total = y_exchange(p, f, b, total)
        a_start(p, observe(ocean * after_y(e, x)))
        return lane_total(total)

    for buf in (xs1, xs2):
        buf[...] = jnp.zeros(buf.shape, F32)
    block = lax.broadcasted_iota(jnp.int32, (1, LANE), 1) // slots
    place = lax.rem(lax.broadcasted_iota(jnp.int32, (1, LANE), 1), slots)
    for c in range(nch):
        held = jnp.zeros((1, LANE), jnp.int32)
        for i in range(per):
            held = jnp.where(block == i, count[:, per * c + i : per * c + i + 1], held)
        occ[c] = jnp.where(place < held, 1.0, 0.0)
    chunks = weigh([line_up(innov, c) for c in range(nch)])
    pl.semaphore_wait(barrier, nodes - 1)
    a_start(0, chunks)

    ti = lax.broadcasted_iota(jnp.int32, (LANE, LANE), 0)
    tj = lax.broadcasted_iota(jnp.int32, (LANE, LANE), 1)
    for k in range(3):
        tri[0, k * LANE : (k + 1) * LANE] = jnp.where(ti <= tj, 1.0, 0.0).astype(BF16)
        tri[1, k * LANE : (k + 1) * LANE] = jnp.where(ti > tj, 1.0, 0.0).astype(BF16)

    rate = rx[...]
    c = sums_x(rate, False)
    p, b = coefficients(cx, shape_of(rate), c, c[:, SUB - 1 :, :], sums_x_after)
    put_rows(ob, jnp.stack([p] * TR))
    put_rows(qb, jnp.stack([b] * TR))
    x_fill(NXP, zero_row)
    x_start(xs1, xr1, x1_ss, x1_rs, NXP)

    def after(a):
        later = sums_y(a, 1)
        return later + a, later

    rate = ry[...]
    c = sums_y(rate, 0)
    p, b = coefficients(cy, shape_of(rate), c, c[:, :, LANE - 1 :], after)
    p = jnp.broadcast_to(p[None], four)
    b = jnp.broadcast_to(b[None], four)
    y_start(NXP, pick(p, LANE - 1), pick(b, 0), zero_row)
    onehots()
    y_wait(NXP)
    x_wait(xs1, xr1, x1_ss, x1_rs, NXP)
    xown[...] = xr1[NXP]
    whole = xown[0, 0:R]
    for j in range(1, nx):
        whole = whole * xown[j, 0:R]
    xinv[0:R] = 1.0 / (1.0 - whole)

    right, _ = forth(0, zero_row)
    res[...] = right
    rr_part = inner(right, right)
    rr = None
    for it in range(ITERS):
        rr_old = rr
        rr = back(2 * it + 1, rr_part)
        if it == 0:
            direction = res[...]
        else:
            direction = res[...] + (rr / rr_old) * drn[...]
        drn[...] = direction
        dd = inner(direction, direction)
        y = a_wait(2 * it + 1)
        if it > 0:
            y = y + (rr / rr_old) * yold[...]
        yold[...] = y
        chunks = weigh(y)
        a_start(2 * it + 2, chunks)
        for k in range(nch):
            dd = dd + y[k] * chunks[k]
        term, total = forth(2 * it + 2, dd)
        alpha = rr / total
        direction = drn[...]
        sol[...] = alpha * direction if it == 0 else sol[...] + alpha * direction
        new = res[...] - alpha * (direction + term)
        res[...] = new
        if it < ITERS - 1:
            rr_part = inner(new, new)


def on_device(nx, ny, rate_x, rate_y, land_mask, obs_cell, obs_count, innovation, obs_weight):
    lev, sx, sy = rate_x.shape
    slots = obs_cell.shape[2]
    nodes = nx * ny
    nch = nodes * slots // LANE
    lines = TR * lev
    assert (sx, sy) == (SUB, LANE) and lines % nx == 0 and lines <= LANE and LANE % slots == 0
    R = lines // nx
    M = (2 * R + 1 + 7) // 8 * 8
    NXP = 2 * ITERS + 1
    field = (TR, lev, SUB, LANE)
    one = (lev, SUB, LANE)
    vm = pltpu.VMEM
    dma = pltpu.SemaphoreType.DMA
    Rp = (R + 7) // 8 * 8
    return pl.pallas_call(
        functools.partial(kernel, nx, ny, lev, slots),
        out_shape=(jax.ShapeDtypeStruct(field, F32),) * 2,
        in_specs=[pl.BlockSpec(memory_space=vm)] * 7,
        out_specs=(pl.BlockSpec(memory_space=vm),) * 2,
        scratch_shapes=[
            vm(field, F32), vm(field, F32),
            vm((lines * SUB, LANE), F32), vm((lines * SUB, LANE), F32),
            vm((6,) + one, F32), vm((6,) + one, F32), vm((2, 3 * LANE, LANE), BF16),
            vm((lines, LANE), F32), vm((lines, LANE), F32),
            vm((lines * SUB, nch * LANE), BF16), vm((LANE, nch * LANE), F32),
            vm((nch, 1, LANE), F32), vm((nch, 1, LANE), F32),
            vm((Rp, LANE), F32), vm((nx, M, LANE), F32),
            vm((NXP, nch, 1, LANE), F32), vm((NXP, nodes, 1, LANE), F32),
            vm((NXP + 1, nx, M, LANE), F32), vm((NXP + 1, nx, M, LANE), F32),
            vm((NXP, nx, M, LANE), F32), vm((NXP, nx, M, LANE), F32),
            vm((NXP + 1, 3 * SUB, LANE), F32), vm((NXP + 1, ny, 3 * SUB, LANE), F32),
            dma((NXP,)), dma((NXP,)), dma((NXP + 1,)), dma((NXP + 1,)),
            dma((NXP,)), dma((NXP,)), dma((NXP + 1,)), dma((NXP + 1,)),
        ],
        compiler_params=pltpu.CompilerParams(
            collective_id=0, has_side_effects=True, vmem_limit_bytes=56 * 1024 * 1024
        ),
    )(rate_x, rate_y, land_mask, obs_cell, obs_count, innovation, obs_weight)


def solution(mesh):
    placed = (
        P(None, "gx", "gy"),
        P(None, "gx", "gy"),
        P("gx", "gy"),
        P(("gx", "gy"), None, None),
        P(("gx", "gy"), None),
        P(("gx", "gy"), None, None),
        P(("gx", "gy"), None, None, None),
    )
    return jax.shard_map(
        functools.partial(on_device, mesh.shape["gx"], mesh.shape["gy"]),
        mesh=mesh,
        in_specs=placed,
        out_specs=(P(None, None, "gx", "gy"), P(None, None, "gx", "gy")),
        check_vma=False,
    )
```

```python
import functools

import jax
import jax.numpy as jnp
from jax import lax
from jax.experimental import pallas as pl
from jax.experimental.pallas import tpu as pltpu
from jax.sharding import PartitionSpec as P

TR = 2
ITERS = 2
SUB = 8
LANE = 128
MESH = pl.DeviceIdType.MESH
F32 = jnp.float32
BF16 = jnp.bfloat16


HALF = LANE // 2


def stages(lines):
    first = lines * 3 // 5
    return ((0, first), (first, lines))


def x_message(rows, scalar):
    return (2 * rows + scalar + SUB - 1) // SUB * SUB


def split3(a):
    hi = a.astype(BF16)
    rest = a - hi.astype(F32)
    mid = rest.astype(BF16)
    lo = (rest - mid.astype(F32)).astype(BF16)
    return hi, mid, lo


def kernel(
    nx, ny, lev, slots,
    rx, ry, mask_ref, cell, count, innov, wobs,
    sol, res,
    drn, v, ob, qb, cx, cy, tri, w3,
    ex, xx, rows1h, lanes1h, occ, yold, xinv,
    as_, ar, xs1, xr1, xs2, xr2, ys, yr,
    a_ss, a_rs, x1_ss, x1_rs, x2_ss, x2_rs, y_ss, y_rs,
):
    nodes = nx * ny
    per = LANE // slots
    nch = nodes * slots // LANE
    lines = TR * lev
    bounds = stages(lines)
    NS = len(bounds)
    mx = lax.axis_index("gx")
    my = lax.axis_index("gy")
    me = mx * ny + my
    NXP = 2 * ITERS + 1
    gxs = [lax.rem(mx + j, nx) for j in range(nx)]
    gys = [lax.rem(my + j, ny) for j in range(ny)]
    others = [(i, j) for i in range(nx) for j in range(ny) if i or j]

    barrier = pltpu.get_barrier_semaphore()
    for i, j in others:
        pl.semaphore_signal(barrier, inc=1, device_id=(gxs[i], gys[j]), device_id_type=MESH)

    three = (lines, SUB, LANE)
    sub_i = lax.broadcasted_iota(jnp.int32, (SUB, LANE), 0)
    lane_i = lax.broadcasted_iota(jnp.int32, (SUB, LANE), 1)
    ocean = mask_ref[...].astype(F32)

    def sums_x(a, back):
        ax = a.ndim - 2
        for s in (1, 2, 4):
            if back:
                a = a + jnp.where(sub_i < SUB - s, pltpu.roll(a, SUB - s, ax), 0.0)
            else:
                a = a + jnp.where(sub_i >= s, pltpu.roll(a, s, ax), 0.0)
        return a

    def sums_x_after(a):
        b = sums_x(a, True)
        return b, jnp.where(sub_i < SUB - 1, pltpu.roll(b, SUB - 1, a.ndim - 2), 0.0)

    def sums_y(a, which):
        flat = a.reshape(a.size // LANE, LANE)
        lhs = jnp.concatenate(split3(flat), axis=1)
        return jnp.dot(lhs, tri[which], preferred_element_type=F32).reshape(a.shape)

    def shape_of(rate):
        decay = jnp.exp(-rate)
        series = 1.0
        for k in (9, 8, 7, 6, 5, 4, 3, 2):
            series = 1.0 - series * rate * (1.0 / k)
        one_minus = rate * series
        return jnp.sqrt(one_minus * (1.0 + decay)) * jnp.sqrt(jnp.sqrt(one_minus))

    def coefficients(co, w, c, end, after):
        p = jnp.exp(-c)
        pinv = jnp.exp(c)
        p2 = p * p
        total, later = after(p2)
        co[0] = w * pinv
        co[1] = p
        co[2] = w * p
        co[3] = p2
        co[4] = w * (p + pinv * later)
        co[5] = w * jnp.exp(c - end)
        return p, total

    def put_rows(ref, a, s):
        t0, t1 = bounds[s]
        ref[t0 * SUB : t1 * SUB] = a.reshape((t1 - t0) * SUB, LANE)

    def of_lines(a, s):
        t0, t1 = bounds[s]
        parts = []
        while t0 < t1:
            low = t0 % lev
            n = min(t1 - t0, lev - low)
            parts.append(a[low : low + n])
            t0 += n
        return parts[0] if len(parts) == 1 else jnp.concatenate(parts, axis=0)

    def local_x(u, s):
        cs = [of_lines(cx[k], s) for k in range(4)]
        f = sums_x(u * cs[0], False)
        total, later = sums_x_after(f * cs[3])
        v[bounds[s][0] : bounds[s][1]] = cs[2] * f + cs[0] * later
        put_rows(ob, cs[1] * f, s)
        put_rows(qb, total, s)

    def pick(a, col, s, shift):
        n = bounds[s][1] - bounds[s][0]
        tag = lax.broadcasted_iota(jnp.int32, (n, SUB, LANE), 2) - lax.broadcasted_iota(jnp.int32, (n, SUB, LANE), 0)
        column = jnp.broadcast_to(a[..., col : col + 1], a.shape)
        return jnp.sum(jnp.where(tag == shift, column, 0.0), axis=0)

    def local_y(u, s):
        cs = [of_lines(cy[k], s) for k in range(4)]
        f = sums_y(u * cs[0], 0)
        m = f * cs[3]
        later = sums_y(m, 1)
        v[bounds[s][0] : bounds[s][1]] = cs[2] * f + cs[0] * later
        return pick(cs[1] * f, LANE - 1, s, 0) + pick(later + m, 0, s, HALF)

    def after_x(s):
        t0, t1 = bounds[s]

        def rows(ref):
            return ref[t0:t1].reshape(t1 - t0, 1, LANE)

        return v[t0:t1] + of_lines(cx[4], s) * rows(ex) + of_lines(cx[5], s) * rows(xx)

    def after_y(e, x, s):
        t0, t1 = bounds[s]

        def columns(a):
            return jnp.stack([jnp.broadcast_to(a[:, t : t + 1], (SUB, LANE)) for t in range(t1 - t0)])

        return v[t0:t1] + of_lines(cy[4], s) * columns(e) + of_lines(cy[5], s) * columns(x)

    zero = jnp.zeros((SUB, LANE), F32)
    zero_row = jnp.zeros((1, LANE), F32)

    def wait_all(buf, sem):
        pltpu.make_async_copy(buf, buf, sem).wait()

    def x_rows(s):
        r = (bounds[s][1] - bounds[s][0]) // nx
        return r, x_message(r, s == 0)

    def x_copies(src, dst, ss, rs, q, s):
        m = x_rows(s)[1]
        for i in range(1, nx):
            pltpu.make_async_remote_copy(
                src_ref=src.at[q, gxs[i], pl.ds(0, m)], dst_ref=dst.at[q, mx, pl.ds(0, m)],
                send_sem=ss.at[q], recv_sem=rs.at[q],
                device_id=(gxs[i], my), device_id_type=MESH,
            ).start()
        dst[q, mx] = src[q, mx]

    def x_wait(dst, ss, rs, q, s):
        m = x_rows(s)[1]
        wait_all(dst.at[q, pl.ds(0, nx - 1), pl.ds(0, m)], rs.at[q])
        wait_all(dst.at[q, pl.ds(0, nx - 1), pl.ds(0, m)], ss.at[q])

    def x_send(p, s, row=None):
        q = NS * p + s
        r = x_rows(s)[0]
        t0 = bounds[s][0]
        for j in range(nx):
            xs1[q, j, 0:r] = ob[pl.ds(SUB - 1 + SUB * (t0 + r * j), r, stride=SUB), :]
            xs1[q, j, r : 2 * r] = qb[pl.ds(SUB * (t0 + r * j), r, stride=SUB), :]
            if row is not None:
                xs1[q, j, 2 * r : 2 * r + 1] = row
        x_copies(xs1, xr1, x1_ss, x1_rs, q, s)

    def x_solve(p, s):
        q = NS * p + s
        k = NS * NXP + s
        r = x_rows(s)[0]
        x_wait(xr1, x1_ss, x1_rs, q, s)
        A = [xr1[k, j, 0:r] for j in range(nx)]
        C = [xr1[k, j, r : 2 * r] for j in range(nx)]
        F = [xr1[q, j, 0:r] for j in range(nx)]
        B = [xr1[q, j, r : 2 * r] for j in range(nx)]
        inv = xinv[s, 0:r]
        e = F[0]
        for j in range(1, nx):
            e = F[j] + A[j] * e
        e = e * inv
        gs = []
        for j in range(nx):
            xs2[q, j, 0:r] = e
            gs.append(B[j] + C[j] * e)
            e = F[j] + A[j] * e
        x = gs[nx - 1]
        for j in range(nx - 2, -1, -1):
            x = gs[j] + A[j] * x
        x = x * inv
        for j in range(nx - 1, -1, -1):
            xs2[q, j, r : 2 * r] = x
            x = gs[j] + A[j] * x
        x_copies(xs2, xr2, x2_ss, x2_rs, q, s)
        if s == 0:
            total = xr1[q, 0, 2 * r : 2 * r + 1]
            for j in range(1, nx):
                total = total + xr1[q, j, 2 * r : 2 * r + 1]
            return total

    def x_finish(p, s):
        q = NS * p + s
        r = x_rows(s)[0]
        t0 = bounds[s][0]
        x_wait(xr2, x2_ss, x2_rs, q, s)
        for j in range(nx):
            ex[t0 + r * j : t0 + r * (j + 1)] = xr2[q, j, 0:r]
            xx[t0 + r * j : t0 + r * (j + 1)] = xr2[q, j, r : 2 * r]

    def y_send(p, s, tile, total=None):
        q = NS * p + s
        if total is not None:
            tile = jnp.where(lane_i == LANE - 1, total, tile)
        ys[q] = tile
        for j in range(1, ny):
            pltpu.make_async_remote_copy(
                src_ref=ys.at[q], dst_ref=yr.at[q, my], send_sem=y_ss.at[q], recv_sem=y_rs.at[q],
                device_id=(mx, gys[j]), device_id_type=MESH,
            ).start()
        yr[q, my] = tile

    def y_wait(q):
        wait_all(yr.at[q, pl.ds(0, ny - 1)], y_rs.at[q])
        wait_all(yr.at[q, pl.ds(0, ny - 1)], y_ss.at[q])

    def y_finish(p, s):
        q = NS * p + s
        k = NS * NXP + s
        y_wait(q)
        tiles = [yr[q, j] for j in range(ny)]
        keeps = [yr[k, j] for j in range(ny)]
        e, mine_e, gs = zero, zero, []
        for j in range(ny):
            mine_e = jnp.where(my == j, e, mine_e)
            gs.append(pltpu.roll(tiles[j], HALF, 1) + pltpu.roll(keeps[j], HALF, 1) * e)
            e = tiles[j] + keeps[j] * e
        x, mine_x = zero, zero
        for j in range(ny - 1, -1, -1):
            mine_x = jnp.where(my == j, x, mine_x)
            x = gs[j] + keeps[j] * x
        total = tiles[0]
        for j in range(1, ny):
            total = total + tiles[j]
        return mine_e, mine_x, jnp.broadcast_to(total[0:1, LANE - 1 : LANE], (1, LANE))

    def a_start(p, chunks):
        for c in range(nch):
            as_[p, c] = chunks[c]
        for i, j in others:
            pltpu.make_async_remote_copy(
                src_ref=as_.at[p, (gxs[i] * ny + gys[j]) // per], dst_ref=ar.at[p, me],
                send_sem=a_ss.at[p], recv_sem=a_rs.at[p],
                device_id=(gxs[i], gys[j]), device_id_type=MESH,
            ).start()
        ar[p, me] = as_[p, me // per]

    def a_wait(p):
        wait_all(ar.at[p, pl.ds(0, nodes - 1)], a_rs.at[p])
        wait_all(ar.at[p, pl.ds(0, nodes - 1)], a_ss.at[p])
        got = ar[p].reshape(nch, per, 1, LANE)
        block = lax.broadcasted_iota(jnp.int32, (nch, 1, LANE), 2) // slots
        mine = lax.rem(me, per)
        total = jnp.zeros((nch, 1, LANE), F32)
        for i in range(per):
            turned = pltpu.roll(got[:, i], lax.rem(i - mine + per, per) * slots, 2)
            total = jnp.where(block == i, turned, total)
        return total

    def line_up(ref, c):
        return jnp.concatenate([ref[0, per * c + i : per * c + i + 1, :] for i in range(per)], axis=1)

    def weigh(y):
        per_block = wobs.shape[2] // LANE
        chunks = []
        for n in range(wobs.shape[1]):
            row = jnp.concatenate([y[per_block * n + a] * occ[per_block * n + a] for a in range(per_block)], axis=1)
            which = lax.broadcasted_iota(jnp.int32, (2 * SUB, row.shape[1]), 0)
            lhs = jnp.zeros(which.shape, F32)
            for k, part in enumerate(split3(row)):
                lhs = jnp.where(which == k, part.astype(F32), lhs)
            lhs = lhs.astype(BF16)
            z = jnp.dot(lhs, w3[n, 2], preferred_element_type=F32)
            z = z + jnp.dot(lhs, w3[n, 1], preferred_element_type=F32)
            z = z + jnp.dot(lhs, w3[n, 0], preferred_element_type=F32)
            z = jnp.sum(z, axis=0, keepdims=True)
            for a in range(per_block):
                chunks.append(z[0:1, a * LANE : (a + 1) * LANE] * occ[per_block * n + a])
        return chunks

    def onehots():
        ri = lax.broadcasted_iota(jnp.int32, (lines * SUB, LANE), 0)
        li = lax.broadcasted_iota(jnp.int32, (LANE, LANE), 0)
        for c in range(nch):
            here = line_up(cell, c)
            cols = slice(c * LANE, (c + 1) * LANE)
            rows1h[:, cols] = jnp.where(ri == here // LANE, 1.0, 0.0).astype(BF16)
            lanes1h[:, cols] = jnp.where(li == lax.rem(here, LANE), 1.0, 0.0)

    def observe(field):
        t = jnp.transpose(field.reshape(lines * SUB, LANE))
        lhs = jnp.concatenate(split3(t), axis=0)
        chunks = []
        for c in range(0, nch, 2):
            wide = min(2, nch - c)
            cols = slice(c * LANE, (c + wide) * LANE)
            got = jnp.dot(lhs, rows1h[:, cols], preferred_element_type=F32)
            got = (got[0:LANE] + got[LANE : 2 * LANE]) + got[2 * LANE :]
            got = jnp.sum(got * lanes1h[:, cols], axis=0, keepdims=True)
            chunks += [got[:, k * LANE : (k + 1) * LANE] for k in range(wide)]
        return chunks

    def deposit(vals):
        row = jnp.concatenate([vals[c] for c in range(nch)], axis=1)
        spread = lanes1h[...]
        rhs = jnp.concatenate([(spread * part.astype(F32)).astype(BF16) for part in split3(row)], axis=0)
        got = lax.dot_general(rows1h[...], rhs, (((1,), (1,)), ((), ())), preferred_element_type=F32)
        got = (got[:, 0:LANE] + got[:, LANE : 2 * LANE]) + got[:, 2 * LANE :]
        return got.reshape(three)

    def lane_total(row):
        return jnp.broadcast_to(jnp.sum(row, axis=1, keepdims=True), (1, LANE))

    def inner(a, b):
        return jnp.sum(jnp.sum(a * b, axis=0), axis=0, keepdims=True)

    every = range(NS)

    def part(ref, s):
        return ref.at[bounds[s][0] : bounds[s][1]]

    def forth_y(p, row):
        field = deposit(a_wait(p))
        for s in every:
            tile = local_y(ocean * field[bounds[s][0] : bounds[s][1]], s)
            y_send(p, s, tile, lane_total(row) if s == 0 else None)

    def forth_x(p):
        total = None
        for s in every:
            e, x, t = y_finish(p, s)
            local_x(after_y(e, x, s), s)
            x_send(p, s, t if s == 0 else None)
        for s in every:
            t = x_solve(p, s)
            total = t if s == 0 else total
        return total

    def back(p, row, beside):
        for s in every:
            local_x(ocean * part(res, s)[...], s)
            x_send(p, s, row if s == 0 else None)
        beside()
        total = None
        for s in every:
            t = x_solve(p, s)
            total = lane_total(t) if s == 0 else total
        for s in every:
            x_finish(p, s)
            y_send(p, s, local_y(after_x(s), s), total if s == 0 else None)
        fields = []
        for s in every:
            e, x, t = y_finish(p, s)
            fields.append(ocean * after_y(e, x, s))
            total = t if s == 0 else total
        a_start(p, observe(jnp.concatenate(fields, axis=0)))
        return total

    for buf in (xs1, xs2):
        buf[...] = jnp.zeros(buf.shape, F32)
    block = lax.broadcasted_iota(jnp.int32, (1, LANE), 1) // slots
    place = lax.rem(lax.broadcasted_iota(jnp.int32, (1, LANE), 1), slots)
    for c in range(nch):
        held = jnp.zeros((1, LANE), jnp.int32)
        for i in range(per):
            held = jnp.where(block == i, count[:, per * c + i : per * c + i + 1], held)
        occ[c] = jnp.where(place < held, 1.0, 0.0)
    for n in range(wobs.shape[1]):
        for k, piece in enumerate(split3(wobs[0, n])):
            w3[n, k] = piece
    chunks = weigh([line_up(innov, c) for c in range(nch)])
    pl.semaphore_wait(barrier, nodes - 1)
    a_start(0, chunks)

    ti = lax.broadcasted_iota(jnp.int32, (LANE, LANE), 0)
    tj = lax.broadcasted_iota(jnp.int32, (LANE, LANE), 1)
    for k in range(3):
        tri[0, k * LANE : (k + 1) * LANE] = jnp.where(ti <= tj, 1.0, 0.0).astype(BF16)
        tri[1, k * LANE : (k + 1) * LANE] = jnp.where(ti > tj, 1.0, 0.0).astype(BF16)

    def after(a):
        later = sums_y(a, 1)
        return later + a, later

    rate = ry[...]
    c = sums_y(rate, 0)
    p, b = coefficients(cy, shape_of(rate), c, c[:, :, LANE - 1 :], after)
    for s in every:
        y_send(NXP, s, pick(of_lines(p, s), LANE - 1, s, 0) + pick(of_lines(b, s), 0, s, HALF))
    onehots()
    forth_y(0, zero_row)
    rate = rx[...]
    c = sums_x(rate, False)
    p, b = coefficients(cx, shape_of(rate), c, c[:, SUB - 1 :, :], sums_x_after)
    for s in every:
        put_rows(ob, of_lines(p, s), s)
        put_rows(qb, of_lines(b, s), s)
        x_send(NXP, s, zero_row if s == 0 else None)
    for s in every:
        y_wait(NS * NXP + s)
    for s in every:
        k = NS * NXP + s
        x_wait(xr1, x1_ss, x1_rs, k, s)
        r = x_rows(s)[0]
        whole = xr1[k, 0, 0:r]
        for j in range(1, nx):
            whole = whole * xr1[k, j, 0:r]
        xinv[s, 0:r] = 1.0 / (1.0 - whole)

    forth_x(0)
    rr_part = zero_row
    for s in every:
        x_finish(0, s)
        right = ocean * after_x(s)
        part(res, s)[...] = right
        rr_part = rr_part + inner(right, right)
    rr = None
    alpha = None
    for it in range(ITERS):
        rr_old = rr

        def beside(alpha=alpha, it=it):
            if it == 1:
                sol[...] = alpha * drn[...]
            elif it > 1:
                sol[...] = sol[...] + alpha * drn[...]

        rr = back(2 * it + 1, rr_part, beside)
        direction = res[...]
        if it > 0:
            direction = direction + (rr / rr_old) * drn[...]
        drn[...] = direction
        dd = inner(direction, direction)
        y = a_wait(2 * it + 1)
        if it > 0:
            y = y + (rr / rr_old) * yold[...]
        yold[...] = y
        chunks = weigh(y)
        a_start(2 * it + 2, chunks)
        for k in range(nch):
            dd = dd + y[k] * chunks[k]
        forth_y(2 * it + 2, dd)
        total = forth_x(2 * it + 2)
        alpha = rr / total
        rr_part = zero_row
        for s in every:
            x_finish(2 * it + 2, s)
            new = part(res, s)[...] - alpha * (part(drn, s)[...] + ocean * after_x(s))
            part(res, s)[...] = new
            if it < ITERS - 1:
                rr_part = rr_part + inner(new, new)
        if it == ITERS - 1:
            last = alpha * drn[...]
            sol[...] = last if it == 0 else sol[...] + last


def on_device(nx, ny, rate_x, rate_y, land_mask, obs_cell, obs_count, innovation, obs_weight):
    lev, sx, sy = rate_x.shape
    slots = obs_cell.shape[2]
    nodes = nx * ny
    nch = nodes * slots // LANE
    lines = TR * lev
    assert (sx, sy) == (SUB, LANE) and lines % nx == 0 and lines <= LANE and LANE % slots == 0
    bounds = stages(lines)
    NS = len(bounds)
    rows = [(b - a) // nx for a, b in bounds]
    assert all((b - a) % nx == 0 and b - a < HALF for a, b in bounds)
    M = max(x_message(r, s == 0) for s, r in enumerate(rows))
    Q = NS * (2 * ITERS + 2)
    NXP = 2 * ITERS + 1
    field = (lines, SUB, LANE)
    one = (lev, SUB, LANE)
    vm = pltpu.VMEM
    dma = pltpu.SemaphoreType.DMA
    Rp = (max(rows) + 7) // 8 * 8
    nb, rb = obs_weight.shape[1:3]
    solved, left = pl.pallas_call(
        functools.partial(kernel, nx, ny, lev, slots),
        out_shape=(jax.ShapeDtypeStruct(field, F32),) * 2,
        in_specs=[pl.BlockSpec(memory_space=vm)] * 7,
        out_specs=(pl.BlockSpec(memory_space=vm),) * 2,
        scratch_shapes=[
            vm(field, F32), vm(field, F32),
            vm((lines * SUB, LANE), F32), vm((lines * SUB, LANE), F32),
            vm((6,) + one, F32), vm((6,) + one, F32), vm((2, 3 * LANE, LANE), BF16),
            vm((nb, 3, rb, rb), BF16),
            vm((lines, LANE), F32), vm((lines, LANE), F32),
            vm((lines * SUB, nch * LANE), BF16), vm((LANE, nch * LANE), F32),
            vm((nch, 1, LANE), F32), vm((nch, 1, LANE), F32),
            vm((NS, Rp, LANE), F32),
            vm((NXP, nch, 1, LANE), F32), vm((NXP, nodes, 1, LANE), F32),
            vm((Q, nx, M, LANE), F32), vm((Q, nx, M, LANE), F32),
            vm((Q, nx, M, LANE), F32), vm((Q, nx, M, LANE), F32),
            vm((Q, SUB, LANE), F32), vm((Q, ny, SUB, LANE), F32),
            dma((NXP,)), dma((NXP,)), dma((Q,)), dma((Q,)),
            dma((Q,)), dma((Q,)), dma((Q,)), dma((Q,)),
        ],
        compiler_params=pltpu.CompilerParams(
            collective_id=0, has_side_effects=True, vmem_limit_bytes=56 * 1024 * 1024
        ),
    )(rate_x, rate_y, land_mask, obs_cell, obs_count, innovation, obs_weight)
    shape = (TR, lev, SUB, LANE)
    return solved.reshape(shape), left.reshape(shape)


def solution(mesh):
    placed = (
        P(None, "gx", "gy"),
        P(None, "gx", "gy"),
        P("gx", "gy"),
        P(("gx", "gy"), None, None),
        P(("gx", "gy"), None),
        P(("gx", "gy"), None, None),
        P(("gx", "gy"), None, None, None),
    )
    return jax.shard_map(
        functools.partial(on_device, mesh.shape["gx"], mesh.shape["gy"]),
        mesh=mesh,
        in_specs=placed,
        out_specs=(P(None, None, "gx", "gy"), P(None, None, "gx", "gy")),
        check_vma=False,
    )
```

```python
import functools

import jax
import jax.numpy as jnp
from jax import lax
from jax.experimental import pallas as pl
from jax.experimental.pallas import tpu as pltpu
from jax.sharding import PartitionSpec as P

TR = 2
ITERS = 2
SUB = 8
LANE = 128
MESH = pl.DeviceIdType.MESH
F32 = jnp.float32
BF16 = jnp.bfloat16


def split3(a):
    hi = a.astype(BF16)
    rest = a - hi.astype(F32)
    mid = rest.astype(BF16)
    lo = (rest - mid.astype(F32)).astype(BF16)
    return hi, mid, lo


def kernel(
    nx, ny, lev, slots,
    rx, ry, mask_ref, cell, count, innov, wobs,
    sol, res,
    drn, v, v2, vy, ob, qb, ob2, qb2, cx, cy, tri, w3,
    states, rows1h, lanes1h, occ, ydir, yres, xinv,
    as_, ar, xs1, xr1, xs2, xr2, xcs, xcr, ys, yr,
    a_ss, a_rs, x1_ss, x1_rs, x2_ss, x2_rs, xc_ss, xc_rs, y_ss, y_rs,
):
    nodes = nx * ny
    per = LANE // slots
    nch = nodes * slots // LANE
    lines = TR * lev
    R = lines // nx
    mx = lax.axis_index("gx")
    my = lax.axis_index("gy")
    me = mx * ny + my
    NXP = 2 * ITERS + 1
    gxs = [lax.rem(mx + j, nx) for j in range(nx)]
    gys = [lax.rem(my + j, ny) for j in range(ny)]
    others = [(i, j) for i in range(nx) for j in range(ny) if i or j]

    barrier = pltpu.get_barrier_semaphore()
    for i, j in others:
        pl.semaphore_signal(barrier, inc=1, device_id=(gxs[i], gys[j]), device_id_type=MESH)

    one = (lev, SUB, LANE)
    four = (TR, lev, SUB, LANE)
    sub_i = lax.broadcasted_iota(jnp.int32, (SUB, LANE), 0)
    lane_i = lax.broadcasted_iota(jnp.int32, (SUB, LANE), 1)
    ocean = mask_ref[...].astype(F32)

    def sums_x(a, back):
        ax = a.ndim - 2
        for s in (1, 2, 4):
            if back:
                a = a + jnp.where(sub_i < SUB - s, pltpu.roll(a, SUB - s, ax), 0.0)
            else:
                a = a + jnp.where(sub_i >= s, pltpu.roll(a, s, ax), 0.0)
        return a

    def sums_x_after(a):
        b = sums_x(a, True)
        return b, jnp.where(sub_i < SUB - 1, pltpu.roll(b, SUB - 1, a.ndim - 2), 0.0)

    def sums_y(a, which):
        flat = a.reshape(a.size // LANE, LANE)
        lhs = jnp.concatenate(split3(flat), axis=1)
        return jnp.dot(lhs, tri[which], preferred_element_type=F32).reshape(a.shape)

    def shape_of(rate):
        decay = jnp.exp(-rate)
        series = 1.0
        for k in (9, 8, 7, 6, 5, 4, 3, 2):
            series = 1.0 - series * rate * (1.0 / k)
        one_minus = rate * series
        return jnp.sqrt(one_minus * (1.0 + decay)) * jnp.sqrt(jnp.sqrt(one_minus))

    def coefficients(co, w, c, end, after):
        p = jnp.exp(-c)
        pinv = jnp.exp(c)
        p2 = p * p
        total, later = after(p2)
        co[0] = w * pinv
        co[1] = p
        co[2] = w * p
        co[3] = p2
        co[4] = w * (p + pinv * later)
        co[5] = w * jnp.exp(c - end)
        return p, total

    def put_rows(ref, a):
        ref[...] = a.reshape(lines * SUB, LANE)

    def solve_x(u):
        s = sums_x(u * cx[0], False)
        total, later = sums_x_after(s * cx[3])
        return cx[2] * s + cx[0] * later, cx[1] * s, total

    def local_x(u, full):
        field, f, b = solve_x(u)
        v[...] = field
        put_rows(ob, f)
        put_rows(qb, b)
        if full:
            field, f, b = solve_x(ocean * ocean * field)
            v2[...] = field
            put_rows(ob2, f)
            put_rows(qb2, b)

    tag = (
        lax.broadcasted_iota(jnp.int32, four, 3)
        - lax.broadcasted_iota(jnp.int32, four, 0) * lev
        - lax.broadcasted_iota(jnp.int32, four, 1)
    )

    def pick(a, col):
        column = jnp.broadcast_to(a[..., col : col + 1], four)
        return jnp.sum(jnp.where(tag == 0, column, 0.0), axis=(0, 1))

    def local_y(u):
        s = sums_y(u * cy[0], 0)
        m = s * cy[3]
        later = sums_y(m, 1)
        vy[...] = cy[2] * s + cy[0] * later
        return pick(cy[1] * s, LANE - 1), pick(later + m, 0)

    def rows(k):
        return states[k].reshape(TR, lev, 1, LANE)

    def after_x():
        return v[...] + cx[4] * rows(0) + cx[5] * rows(1)

    def after_xx():
        return v2[...] + cx[6] * rows(0) + cx[7] * rows(1) + cx[4] * rows(2) + cx[5] * rows(3)

    def after_y(e, x):
        def columns(a):
            parts = [jnp.broadcast_to(a[:, t : t + 1], (SUB, LANE)) for t in range(lines)]
            return jnp.stack(parts).reshape(four)

        return vy[...] + cy[4] * columns(e) + cy[5] * columns(x)

    zero = jnp.zeros((SUB, LANE), F32)
    zero_row = jnp.zeros((1, LANE), F32)

    def wait_all(buf, sem):
        pltpu.make_async_copy(buf, buf, sem).wait()

    def x_start(src, dst, ss, rs, p, m):
        for i in range(1, nx):
            pltpu.make_async_remote_copy(
                src_ref=src.at[p, gxs[i], pl.ds(0, m)], dst_ref=dst.at[p, mx, pl.ds(0, m)],
                send_sem=ss.at[p], recv_sem=rs.at[p],
                device_id=(gxs[i], my), device_id_type=MESH,
            ).start()
        dst[p, mx] = src[p, mx]

    def x_wait(dst, ss, rs, p, m):
        wait_all(dst.at[p, pl.ds(0, nx - 1), pl.ds(0, m)], rs.at[p])
        wait_all(dst.at[p, pl.ds(0, nx - 1), pl.ds(0, m)], ss.at[p])

    def edge(ref, j, last):
        return ref[pl.ds((SUB - 1 if last else 0) + SUB * R * j, R, stride=SUB), :]

    def x_exchange(p, full):
        m = (R * (4 if full else 2) + SUB - 1) // SUB * SUB
        for j in range(nx):
            xs1[p, j, 0:R] = edge(ob, j, True)
            xs1[p, j, R : 2 * R] = edge(qb, j, False)
            if full:
                xs1[p, j, 2 * R : 3 * R] = edge(ob2, j, True)
                xs1[p, j, 3 * R : 4 * R] = edge(qb2, j, False)
        x_start(xs1, xr1, x1_ss, x1_rs, p, m)
        x_wait(xr1, x1_ss, x1_rs, p, m)

        def got(k):
            return [xr1[p, j, k * R : (k + 1) * R] for j in range(nx)]

        def kept(k):
            return [xcr[0, j, k * R : (k + 1) * R] for j in range(nx)]

        A, C = kept(0), kept(1)
        inv = xinv[0:R]

        def chain(F, B):
            e = F[0]
            for j in range(1, nx):
                e = F[j] + A[j] * e
            e = e * inv
            es, gs, out = [], [], [None] * nx
            for j in range(nx):
                es.append(e)
                gs.append(B[j] + C[j] * e)
                e = F[j] + A[j] * e
            x = gs[nx - 1]
            for j in range(nx - 2, -1, -1):
                x = gs[j] + A[j] * x
            x = x * inv
            for j in range(nx - 1, -1, -1):
                out[j] = x
                x = gs[j] + A[j] * x
            return es, out

        found = list(chain(got(0), got(1)))
        if full:
            es, out = found
            F = [f + a * e + b * x for f, a, b, e, x in zip(got(2), kept(2), kept(3), es, out)]
            B = [f + a * e + b * x for f, a, b, e, x in zip(got(3), kept(4), kept(5), es, out)]
            found += chain(F, B)
        for k, values in enumerate(found):
            for j in range(nx):
                xs2[p, j, k * R : (k + 1) * R] = values[j]
        x_start(xs2, xr2, x2_ss, x2_rs, p, m)
        x_wait(xr2, x2_ss, x2_rs, p, m)
        for k in range(len(found)):
            for j in range(nx):
                states[k, R * j : R * (j + 1)] = xr2[p, j, k * R : (k + 1) * R]

    def y_start(p, f, b):
        ys[p, 0:SUB] = f
        ys[p, SUB : 2 * SUB] = b
        for j in range(1, ny):
            pltpu.make_async_remote_copy(
                src_ref=ys.at[p], dst_ref=yr.at[p, my], send_sem=y_ss.at[p], recv_sem=y_rs.at[p],
                device_id=(mx, gys[j]), device_id_type=MESH,
            ).start()
        yr[p, my] = ys[p]

    def y_wait(p):
        wait_all(yr.at[p, pl.ds(0, ny - 1)], y_rs.at[p])
        wait_all(yr.at[p, pl.ds(0, ny - 1)], y_ss.at[p])

    def y_finish(p):
        y_wait(p)
        e, mine_e, gs = zero, zero, []
        for j in range(ny):
            mine_e = jnp.where(my == j, e, mine_e)
            gs.append(yr[p, j, SUB : 2 * SUB] + yr[NXP, j, SUB : 2 * SUB] * e)
            e = yr[p, j, 0:SUB] + yr[NXP, j, 0:SUB] * e
        x, mine_x = zero, zero
        for j in range(ny - 1, -1, -1):
            mine_x = jnp.where(my == j, x, mine_x)
            x = gs[j] + yr[NXP, j, 0:SUB] * x
        return mine_e, mine_x

    def a_start(p, chunks, row):
        for c in range(nch):
            as_[p, c, 0:1] = chunks[c]
            as_[p, c, 1:2] = row
        for i, j in others:
            pltpu.make_async_remote_copy(
                src_ref=as_.at[p, (gxs[i] * ny + gys[j]) // per], dst_ref=ar.at[p, me],
                send_sem=a_ss.at[p], recv_sem=a_rs.at[p],
                device_id=(gxs[i], gys[j]), device_id_type=MESH,
            ).start()
        ar[p, me] = as_[p, me // per]

    def a_wait(p):
        wait_all(ar.at[p, pl.ds(0, nodes - 1)], a_rs.at[p])
        wait_all(ar.at[p, pl.ds(0, nodes - 1)], a_ss.at[p])
        got = ar[p, :, 0:1, :].reshape(nch, per, 1, LANE)
        block = lax.broadcasted_iota(jnp.int32, (nch, 1, LANE), 2) // slots
        mine = lax.rem(me, per)
        total = jnp.zeros((nch, 1, LANE), F32)
        for i in range(per):
            turned = pltpu.roll(got[:, i], lax.rem(i - mine + per, per) * slots, 2)
            total = jnp.where(block == i, turned, total)
        row = jnp.sum(ar[p, :, 1:2, :], axis=0)
        return total, jnp.broadcast_to(jnp.sum(row, axis=1, keepdims=True), (1, LANE))

    def line_up(ref, c):
        return jnp.concatenate([ref[0, per * c + i : per * c + i + 1, :] for i in range(per)], axis=1)

    def weigh(y):
        per_block = wobs.shape[2] // LANE
        chunks = []
        for n in range(wobs.shape[1]):
            row = jnp.concatenate([y[per_block * n + a] * occ[per_block * n + a] for a in range(per_block)], axis=1)
            which = lax.broadcasted_iota(jnp.int32, (2 * SUB, row.shape[1]), 0)
            lhs = jnp.zeros(which.shape, F32)
            for k, part in enumerate(split3(row)):
                lhs = jnp.where(which == k, part.astype(F32), lhs)
            lhs = lhs.astype(BF16)
            z = jnp.dot(lhs, w3[n, 2], preferred_element_type=F32)
            z = z + jnp.dot(lhs, w3[n, 1], preferred_element_type=F32)
            z = z + jnp.dot(lhs, w3[n, 0], preferred_element_type=F32)
            z = jnp.sum(z, axis=0, keepdims=True)
            for a in range(per_block):
                chunks.append(z[0:1, a * LANE : (a + 1) * LANE] * occ[per_block * n + a])
        return chunks

    def onehots():
        ri = lax.broadcasted_iota(jnp.int32, (lines * SUB, LANE), 0)
        li = lax.broadcasted_iota(jnp.int32, (LANE, LANE), 0)
        for c in range(nch):
            here = line_up(cell, c)
            cols = slice(c * LANE, (c + 1) * LANE)
            rows1h[:, cols] = jnp.where(ri == here // LANE, 1.0, 0.0).astype(BF16)
            lanes1h[:, cols] = jnp.where(li == lax.rem(here, LANE), 1.0, 0.0)

    def observe(field):
        t = jnp.transpose(field.reshape(lines * SUB, LANE))
        lhs = jnp.concatenate(split3(t), axis=0)
        chunks = []
        for c in range(0, nch, 2):
            wide = min(2, nch - c)
            cols = slice(c * LANE, (c + wide) * LANE)
            got = jnp.dot(lhs, rows1h[:, cols], preferred_element_type=F32)
            got = (got[0:LANE] + got[LANE : 2 * LANE]) + got[2 * LANE :]
            got = jnp.sum(got * lanes1h[:, cols], axis=0, keepdims=True)
            chunks += [got[:, k * LANE : (k + 1) * LANE] for k in range(wide)]
        return chunks

    def deposit(vals):
        row = jnp.concatenate([vals[c] for c in range(nch)], axis=1)
        spread = lanes1h[...]
        rhs = jnp.concatenate([(spread * part.astype(F32)).astype(BF16) for part in split3(row)], axis=0)
        got = lax.dot_general(rows1h[...], rhs, (((1,), (1,)), ((), ())), preferred_element_type=F32)
        got = (got[:, 0:LANE] + got[:, LANE : 2 * LANE]) + got[:, 2 * LANE :]
        return got.reshape(four)

    def inner(a, b):
        return jnp.sum(jnp.sum(a * b, axis=(0, 1)), axis=0, keepdims=True)

    def forth(p, full, beside=None):
        vals, total = a_wait(p)
        y_start(p, *local_y(ocean * deposit(vals)))
        if beside is not None:
            beside()
        local_x(after_y(*y_finish(p)), full)
        x_exchange(p, full)
        return total

    def back(p, beside):
        y_start(p, *local_y(after_xx()))
        row = beside()
        a_start(p, observe(ocean * after_y(*y_finish(p))), row)

    for buf in (xs1, xs2, xcs):
        buf[...] = jnp.zeros(buf.shape, F32)
    block = lax.broadcasted_iota(jnp.int32, (1, LANE), 1) // slots
    place = lax.rem(lax.broadcasted_iota(jnp.int32, (1, LANE), 1), slots)
    for c in range(nch):
        held = jnp.zeros((1, LANE), jnp.int32)
        for i in range(per):
            held = jnp.where(block == i, count[:, per * c + i : per * c + i + 1], held)
        occ[c] = jnp.where(place < held, 1.0, 0.0)
    for n in range(wobs.shape[1]):
        for k, piece in enumerate(split3(wobs[0, n])):
            w3[n, k] = piece
    chunks = weigh([line_up(innov, c) for c in range(nch)])
    pl.semaphore_wait(barrier, nodes - 1)
    a_start(0, chunks, zero_row)

    ti = lax.broadcasted_iota(jnp.int32, (LANE, LANE), 0)
    tj = lax.broadcasted_iota(jnp.int32, (LANE, LANE), 1)
    for k in range(3):
        tri[0, k * LANE : (k + 1) * LANE] = jnp.where(ti <= tj, 1.0, 0.0).astype(BF16)
        tri[1, k * LANE : (k + 1) * LANE] = jnp.where(ti > tj, 1.0, 0.0).astype(BF16)

    def after(a):
        later = sums_y(a, 1)
        return later + a, later

    rate = ry[...]
    c = sums_y(rate, 0)
    p, b = coefficients(cy, shape_of(rate), c, c[:, :, LANE - 1 :], after)
    p = jnp.broadcast_to(p[None], four)
    b = jnp.broadcast_to(b[None], four)
    y_start(NXP, pick(p, LANE - 1), pick(b, 0))
    onehots()

    def prepare_x():
        rate = rx[...]
        c = sums_x(rate, False)
        p, b = coefficients(cx, shape_of(rate), c, c[:, SUB - 1 :, :], sums_x_after)
        cx[6], f4, b4 = solve_x(ocean * ocean * cx[4])
        cx[7], f5, b5 = solve_x(ocean * ocean * cx[5])
        for k, (a, last) in enumerate(((p, 1), (b, 0), (f4, 1), (f5, 1), (b4, 0), (b5, 0))):
            buf = (ob, qb)[k % 2]
            put_rows(buf, jnp.stack([a] * TR))
            for j in range(nx):
                xcs[0, j, k * R : (k + 1) * R] = edge(buf, j, last)
        x_start(xcs, xcr, xc_ss, xc_rs, 0, xcs.shape[2])
        y_wait(NXP)

    def finish_x():
        x_wait(xcr, xc_ss, xc_rs, 0, xcs.shape[2])
        whole = xcr[0, 0, 0:R]
        for j in range(1, nx):
            whole = whole * xcr[0, j, 0:R]
        xinv[0:R] = 1.0 / (1.0 - whole)

    vals, _ = a_wait(0)
    y_start(0, *local_y(ocean * deposit(vals)))
    prepare_x()
    local_x(after_y(*y_finish(0)), True)
    finish_x()
    x_exchange(0, True)

    def begin():
        right = ocean * after_x()
        res[...] = right
        drn[...] = right
        return inner(right, right)

    back(1, begin)
    y, rr = a_wait(1)
    ydir[...] = y
    yres[...] = y
    dd = inner(drn[...], drn[...])
    for it in range(ITERS):
        last = it == ITERS - 1
        p = 2 * it + 2
        y = ydir[...]
        chunks = weigh(y)
        row = dd
        for k in range(nch):
            row = row + y[k] * chunks[k]
        a_start(p, chunks, row)
        alpha = rr / forth(p, not last)

        def update():
            d = drn[...]
            sol[...] = alpha * d if it == 0 else sol[...] + alpha * d
            new = res[...] - alpha * (d + ocean * after_x())
            res[...] = new
            return inner(new, new) if not last else None

        if last:
            update()
        else:
            back(p + 1, update)
            t, new_rr = a_wait(p + 1)
            beta = new_rr / rr
            rr = new_rr
            y = yres[...] - alpha * (ydir[...] + t)
            yres[...] = y
            ydir[...] = y + beta * ydir[...]
            d = res[...] + beta * drn[...]
            drn[...] = d
            dd = inner(d, d)


def on_device(nx, ny, rate_x, rate_y, land_mask, obs_cell, obs_count, innovation, obs_weight):
    lev, sx, sy = rate_x.shape
    slots = obs_cell.shape[2]
    nodes = nx * ny
    nch = nodes * slots // LANE
    lines = TR * lev
    assert (sx, sy) == (SUB, LANE) and lines % nx == 0 and lines <= LANE and LANE % slots == 0
    R = lines // nx
    M = (4 * R + 7) // 8 * 8
    MC = (6 * R + 7) // 8 * 8
    NXP = 2 * ITERS + 1
    field = (TR, lev, SUB, LANE)
    one = (lev, SUB, LANE)
    vm = pltpu.VMEM
    dma = pltpu.SemaphoreType.DMA
    Rp = (R + 7) // 8 * 8
    nb, rb = obs_weight.shape[1:3]
    return pl.pallas_call(
        functools.partial(kernel, nx, ny, lev, slots),
        out_shape=(jax.ShapeDtypeStruct(field, F32),) * 2,
        in_specs=[pl.BlockSpec(memory_space=vm)] * 7,
        out_specs=(pl.BlockSpec(memory_space=vm),) * 2,
        scratch_shapes=[
            vm(field, F32), vm(field, F32), vm(field, F32), vm(field, F32),
            vm((lines * SUB, LANE), F32), vm((lines * SUB, LANE), F32),
            vm((lines * SUB, LANE), F32), vm((lines * SUB, LANE), F32),
            vm((8,) + one, F32), vm((6,) + one, F32), vm((2, 3 * LANE, LANE), BF16),
            vm((nb, 3, rb, rb), BF16),
            vm((4, lines, LANE), F32),
            vm((lines * SUB, nch * LANE), BF16), vm((LANE, nch * LANE), F32),
            vm((nch, 1, LANE), F32), vm((nch, 1, LANE), F32), vm((nch, 1, LANE), F32),
            vm((Rp, LANE), F32),
            vm((NXP, nch, 2, LANE), F32), vm((NXP, nodes, 2, LANE), F32),
            vm((NXP, nx, M, LANE), F32), vm((NXP, nx, M, LANE), F32),
            vm((NXP, nx, M, LANE), F32), vm((NXP, nx, M, LANE), F32),
            vm((1, nx, MC, LANE), F32), vm((1, nx, MC, LANE), F32),
            vm((NXP + 1, 2 * SUB, LANE), F32), vm((NXP + 1, ny, 2 * SUB, LANE), F32),
            dma((NXP,)), dma((NXP,)), dma((NXP,)), dma((NXP,)), dma((NXP,)), dma((NXP,)),
            dma((1,)), dma((1,)), dma((NXP + 1,)), dma((NXP + 1,)),
        ],
        compiler_params=pltpu.CompilerParams(
            collective_id=0, has_side_effects=True, vmem_limit_bytes=56 * 1024 * 1024
        ),
    )(rate_x, rate_y, land_mask, obs_cell, obs_count, innovation, obs_weight)


def solution(mesh):
    placed = (
        P(None, "gx", "gy"),
        P(None, "gx", "gy"),
        P("gx", "gy"),
        P(("gx", "gy"), None, None),
        P(("gx", "gy"), None),
        P(("gx", "gy"), None, None),
        P(("gx", "gy"), None, None, None),
    )
    return jax.shard_map(
        functools.partial(on_device, mesh.shape["gx"], mesh.shape["gy"]),
        mesh=mesh,
        in_specs=placed,
        out_specs=(P(None, None, "gx", "gy"), P(None, None, "gx", "gy")),
        check_vma=False,
    )
```

```python
import functools

import jax
import jax.numpy as jnp
from jax import lax
from jax.experimental import pallas as pl
from jax.experimental.pallas import tpu as pltpu
from jax.sharding import PartitionSpec as P

TR = 2
ITERS = 2
SUB = 8
LANE = 128
MESH = pl.DeviceIdType.MESH
F32 = jnp.float32
BF16 = jnp.bfloat16


def split3(a):
    hi = a.astype(BF16)
    rest = a - hi.astype(F32)
    mid = rest.astype(BF16)
    lo = (rest - mid.astype(F32)).astype(BF16)
    return hi, mid, lo


def kernel(
    nx, ny, lev, slots,
    rx, ry, mask_ref, cell, count, innov, wobs,
    sol, res,
    drn, v, v2, vy, ob, qb, ob2, qb2, cx, cy, tri, w3,
    states, rows1h, lanes1h, occ, ydir, yres, xinv,
    as_, ar, xs1, xr1, xs2, xr2, xcs, xcr, ys, yr,
    a_ss, a_rs, x1_ss, x1_rs, x2_ss, x2_rs, xc_ss, xc_rs, y_ss, y_rs,
):
    nodes = nx * ny
    per = LANE // slots
    nch = nodes * slots // LANE
    lines = TR * lev
    R = lines // nx
    mx = lax.axis_index("gx")
    my = lax.axis_index("gy")
    me = mx * ny + my
    NXP = 2 * ITERS + 1
    gxs = [lax.rem(mx + j, nx) for j in range(nx)]
    gys = [lax.rem(my + j, ny) for j in range(ny)]
    others = [(i, j) for i in range(nx) for j in range(ny) if i or j]

    barrier = pltpu.get_barrier_semaphore()
    for i, j in others:
        pl.semaphore_signal(barrier, inc=1, device_id=(gxs[i], gys[j]), device_id_type=MESH)

    one = (lev, SUB, LANE)
    four = (TR, lev, SUB, LANE)
    sub_i = lax.broadcasted_iota(jnp.int32, (SUB, LANE), 0)
    lane_i = lax.broadcasted_iota(jnp.int32, (SUB, LANE), 1)
    ocean = mask_ref[...].astype(F32)

    def sums_x(a, back):
        ax = a.ndim - 2
        for s in (1, 2, 4):
            if back:
                a = a + jnp.where(sub_i < SUB - s, pltpu.roll(a, SUB - s, ax), 0.0)
            else:
                a = a + jnp.where(sub_i >= s, pltpu.roll(a, s, ax), 0.0)
        return a

    def sums_x_after(a):
        b = sums_x(a, True)
        return b, jnp.where(sub_i < SUB - 1, pltpu.roll(b, SUB - 1, a.ndim - 2), 0.0)

    def sums_y(a, which):
        flat = a.reshape(a.size // LANE, LANE)
        lhs = jnp.concatenate(split3(flat), axis=1)
        return jnp.dot(lhs, tri[which], preferred_element_type=F32).reshape(a.shape)

    def shape_of(rate):
        decay = jnp.exp(-rate)
        series = 1.0
        for k in (9, 8, 7, 6, 5, 4, 3, 2):
            series = 1.0 - series * rate * (1.0 / k)
        one_minus = rate * series
        return jnp.sqrt(one_minus * (1.0 + decay)) * jnp.sqrt(jnp.sqrt(one_minus))

    def coefficients(co, w, c, end, after):
        p = jnp.exp(-c)
        pinv = jnp.exp(c)
        p2 = p * p
        total, later = after(p2)
        co[0] = w * pinv
        co[1] = p
        co[2] = w * p
        co[3] = p2
        co[4] = w * (p + pinv * later)
        co[5] = w * jnp.exp(c - end)
        return p, total

    def put_rows(ref, a):
        ref[...] = a.reshape(lines * SUB, LANE)

    def solve_x(u):
        s = sums_x(u * cx[0], False)
        total, later = sums_x_after(s * cx[3])
        return cx[2] * s + cx[0] * later, cx[1] * s, total

    def local_x(u, full):
        field, f, b = solve_x(u)
        v[...] = field
        put_rows(ob, f)
        put_rows(qb, b)
        if full:
            field, f, b = solve_x(ocean * ocean * field)
            v2[...] = field
            put_rows(ob2, f)
            put_rows(qb2, b)

    tag = (
        lax.broadcasted_iota(jnp.int32, four, 3)
        - lax.broadcasted_iota(jnp.int32, four, 0) * lev
        - lax.broadcasted_iota(jnp.int32, four, 1)
    )

    def pick(a, col):
        column = jnp.broadcast_to(a[..., col : col + 1], four)
        return jnp.sum(jnp.where(tag == 0, column, 0.0), axis=(0, 1))

    def local_y(u):
        s = sums_y(u * cy[0], 0)
        m = s * cy[3]
        later = sums_y(m, 1)
        vy[...] = cy[2] * s + cy[0] * later
        return pick(cy[1] * s, LANE - 1), pick(later + m, 0)

    def rows(k):
        return states[k].reshape(TR, lev, 1, LANE)

    def after_x():
        return v[...] + cx[4] * rows(0) + cx[5] * rows(1)

    def after_xx():
        return v2[...] + cx[6] * rows(0) + cx[7] * rows(1) + cx[4] * rows(2) + cx[5] * rows(3)

    def after_y(e, x):
        def columns(a):
            parts = [jnp.broadcast_to(a[:, t : t + 1], (SUB, LANE)) for t in range(lines)]
            return jnp.stack(parts).reshape(four)

        return vy[...] + cy[4] * columns(e) + cy[5] * columns(x)

    zero = jnp.zeros((SUB, LANE), F32)
    zero_row = jnp.zeros((1, LANE), F32)

    def wait_all(buf, sem):
        pltpu.make_async_copy(buf, buf, sem).wait()

    def x_start(src, dst, ss, rs, p, m):
        for i in range(1, nx):
            pltpu.make_async_remote_copy(
                src_ref=src.at[p, gxs[i], pl.ds(0, m)], dst_ref=dst.at[p, mx, pl.ds(0, m)],
                send_sem=ss.at[p], recv_sem=rs.at[p],
                device_id=(gxs[i], my), device_id_type=MESH,
            ).start()
        dst[p, mx] = src[p, mx]

    def x_wait(dst, ss, rs, p, m):
        wait_all(dst.at[p, pl.ds(0, nx - 1), pl.ds(0, m)], rs.at[p])
        wait_all(dst.at[p, pl.ds(0, nx - 1), pl.ds(0, m)], ss.at[p])

    def edge(ref, j, last):
        return ref[pl.ds((SUB - 1 if last else 0) + SUB * R * j, R, stride=SUB), :]

    def x_exchange(p, full):
        m = (R * (4 if full else 2) + SUB - 1) // SUB * SUB
        for j in range(nx):
            xs1[p, j, 0:R] = edge(ob, j, True)
            xs1[p, j, R : 2 * R] = edge(qb, j, False)
            if full:
                xs1[p, j, 2 * R : 3 * R] = edge(ob2, j, True)
                xs1[p, j, 3 * R : 4 * R] = edge(qb2, j, False)
        x_start(xs1, xr1, x1_ss, x1_rs, p, m)
        x_wait(xr1, x1_ss, x1_rs, p, m)

        def got(k):
            return [xr1[p, j, k * R : (k + 1) * R] for j in range(nx)]

        def kept(k):
            return [xcr[0, j, k * R : (k + 1) * R] for j in range(nx)]

        A, C = kept(0), kept(1)
        inv = xinv[0:R]

        def chain(F, B):
            e = F[0]
            for j in range(1, nx):
                e = F[j] + A[j] * e
            e = e * inv
            es, gs, out = [], [], [None] * nx
            for j in range(nx):
                es.append(e)
                gs.append(B[j] + C[j] * e)
                e = F[j] + A[j] * e
            x = gs[nx - 1]
            for j in range(nx - 2, -1, -1):
                x = gs[j] + A[j] * x
            x = x * inv
            for j in range(nx - 1, -1, -1):
                out[j] = x
                x = gs[j] + A[j] * x
            return es, out

        found = list(chain(got(0), got(1)))
        if full:
            es, out = found
            F = [f + a * e + b * x for f, a, b, e, x in zip(got(2), kept(2), kept(3), es, out)]
            B = [f + a * e + b * x for f, a, b, e, x in zip(got(3), kept(4), kept(5), es, out)]
            found += chain(F, B)
        for k, values in enumerate(found):
            for j in range(nx):
                xs2[p, j, k * R : (k + 1) * R] = values[j]
        x_start(xs2, xr2, x2_ss, x2_rs, p, m)
        x_wait(xr2, x2_ss, x2_rs, p, m)
        for k in range(len(found)):
            for j in range(nx):
                states[k, R * j : R * (j + 1)] = xr2[p, j, k * R : (k + 1) * R]

    def y_start(p, f, b):
        ys[p, 0:SUB] = f
        ys[p, SUB : 2 * SUB] = b
        for j in range(1, ny):
            pltpu.make_async_remote_copy(
                src_ref=ys.at[p], dst_ref=yr.at[p, my], send_sem=y_ss.at[p], recv_sem=y_rs.at[p],
                device_id=(mx, gys[j]), device_id_type=MESH,
            ).start()
        yr[p, my] = ys[p]

    def y_wait(p):
        wait_all(yr.at[p, pl.ds(0, ny - 1)], y_rs.at[p])
        wait_all(yr.at[p, pl.ds(0, ny - 1)], y_ss.at[p])

    def y_finish(p):
        y_wait(p)
        e, mine_e, gs = zero, zero, []
        for j in range(ny):
            mine_e = jnp.where(my == j, e, mine_e)
            gs.append(yr[p, j, SUB : 2 * SUB] + yr[NXP, j, SUB : 2 * SUB] * e)
            e = yr[p, j, 0:SUB] + yr[NXP, j, 0:SUB] * e
        x, mine_x = zero, zero
        for j in range(ny - 1, -1, -1):
            mine_x = jnp.where(my == j, x, mine_x)
            x = gs[j] + yr[NXP, j, 0:SUB] * x
        return mine_e, mine_x

    def a_start(p, chunks, row):
        for c in range(nch):
            as_[p, c, 0:1] = chunks[c]
            as_[p, c, 1:2] = row
        for i, j in others:
            pltpu.make_async_remote_copy(
                src_ref=as_.at[p, (gxs[i] * ny + gys[j]) // per], dst_ref=ar.at[p, me],
                send_sem=a_ss.at[p], recv_sem=a_rs.at[p],
                device_id=(gxs[i], gys[j]), device_id_type=MESH,
            ).start()
        ar[p, me] = as_[p, me // per]

    def a_wait(p):
        wait_all(ar.at[p, pl.ds(0, nodes - 1)], a_rs.at[p])
        wait_all(ar.at[p, pl.ds(0, nodes - 1)], a_ss.at[p])
        got = ar[p, :, 0:1, :].reshape(nch, per, 1, LANE)
        block = lax.broadcasted_iota(jnp.int32, (nch, 1, LANE), 2) // slots
        mine = lax.rem(me, per)
        total = jnp.zeros((nch, 1, LANE), F32)
        for i in range(per):
            turned = pltpu.roll(got[:, i], lax.rem(i - mine + per, per) * slots, 2)
            total = jnp.where(block == i, turned, total)
        row = jnp.sum(ar[p, :, 1:2, :], axis=0)
        return total, jnp.broadcast_to(jnp.sum(row, axis=1, keepdims=True), (1, LANE))

    def line_up(ref, c):
        return jnp.concatenate([ref[0, per * c + i : per * c + i + 1, :] for i in range(per)], axis=1)

    def weigh(y):
        per_block = wobs.shape[2] // LANE
        chunks = []
        for n in range(wobs.shape[1]):
            row = jnp.concatenate([y[per_block * n + a] * occ[per_block * n + a] for a in range(per_block)], axis=1)
            which = lax.broadcasted_iota(jnp.int32, (2 * SUB, row.shape[1]), 0)
            lhs = jnp.zeros(which.shape, F32)
            for k, part in enumerate(split3(row)):
                lhs = jnp.where(which == k, part.astype(F32), lhs)
            lhs = lhs.astype(BF16)
            z = jnp.dot(lhs, w3[n, 2], preferred_element_type=F32)
            z = z + jnp.dot(lhs, w3[n, 1], preferred_element_type=F32)
            z = z + jnp.dot(lhs, w3[n, 0], preferred_element_type=F32)
            z = jnp.sum(z, axis=0, keepdims=True)
            for a in range(per_block):
                chunks.append(z[0:1, a * LANE : (a + 1) * LANE] * occ[per_block * n + a])
        return chunks

    def onehots():
        ri = lax.broadcasted_iota(jnp.int32, (lines * SUB, LANE), 0)
        li = lax.broadcasted_iota(jnp.int32, (LANE, LANE), 0)
        for c in range(nch):
            here = line_up(cell, c)
            cols = slice(c * LANE, (c + 1) * LANE)
            rows1h[:, cols] = jnp.where(ri == here // LANE, 1.0, 0.0).astype(BF16)
            lanes1h[:, cols] = jnp.where(li == lax.rem(here, LANE), 1.0, 0.0)

    def observe(field):
        t = jnp.transpose(field.reshape(lines * SUB, LANE))
        lhs = jnp.concatenate(split3(t), axis=0)
        chunks = []
        for c in range(0, nch, 2):
            wide = min(2, nch - c)
            cols = slice(c * LANE, (c + wide) * LANE)
            got = jnp.dot(lhs, rows1h[:, cols], preferred_element_type=F32)
            got = (got[0:LANE] + got[LANE : 2 * LANE]) + got[2 * LANE :]
            got = jnp.sum(got * lanes1h[:, cols], axis=0, keepdims=True)
            chunks += [got[:, k * LANE : (k + 1) * LANE] for k in range(wide)]
        return chunks

    def deposit(vals):
        row = jnp.concatenate([vals[c] for c in range(nch)], axis=1)
        spread = lanes1h[...]
        rhs = jnp.concatenate([(spread * part.astype(F32)).astype(BF16) for part in split3(row)], axis=0)
        got = lax.dot_general(rows1h[...], rhs, (((1,), (1,)), ((), ())), preferred_element_type=F32)
        got = (got[:, 0:LANE] + got[:, LANE : 2 * LANE]) + got[:, 2 * LANE :]
        return got.reshape(four)

    def inner(a, b):
        return jnp.sum(jnp.sum(a * b, axis=(0, 1)), axis=0, keepdims=True)

    def forth(p, full, beside=None):
        vals, total = a_wait(p)
        y_start(p, *local_y(ocean * deposit(vals)))
        if beside is not None:
            beside()
        local_x(after_y(*y_finish(p)), full)
        x_exchange(p, full)
        return total

    def back(p, beside):
        y_start(p, *local_y(after_xx()))
        row = beside()
        a_start(p, observe(ocean * after_y(*y_finish(p))), row)

    for buf in (xs1, xs2, xcs):
        buf[...] = jnp.zeros(buf.shape, F32)
    block = lax.broadcasted_iota(jnp.int32, (1, LANE), 1) // slots
    place = lax.rem(lax.broadcasted_iota(jnp.int32, (1, LANE), 1), slots)
    for c in range(nch):
        held = jnp.zeros((1, LANE), jnp.int32)
        for i in range(per):
            held = jnp.where(block == i, count[:, per * c + i : per * c + i + 1], held)
        occ[c] = jnp.where(place < held, 1.0, 0.0)
    for n in range(wobs.shape[1]):
        for k, piece in enumerate(split3(wobs[0, n])):
            w3[n, k] = piece
    chunks = weigh([line_up(innov, c) for c in range(nch)])
    pl.semaphore_wait(barrier, nodes - 1)
    a_start(0, chunks, zero_row)

    ti = lax.broadcasted_iota(jnp.int32, (LANE, LANE), 0)
    tj = lax.broadcasted_iota(jnp.int32, (LANE, LANE), 1)
    for k in range(3):
        tri[0, k * LANE : (k + 1) * LANE] = jnp.where(ti <= tj, 1.0, 0.0).astype(BF16)
        tri[1, k * LANE : (k + 1) * LANE] = jnp.where(ti > tj, 1.0, 0.0).astype(BF16)

    def after(a):
        later = sums_y(a, 1)
        return later + a, later

    rate = ry[...]
    c = sums_y(rate, 0)
    p, b = coefficients(cy, shape_of(rate), c, c[:, :, LANE - 1 :], after)
    p = jnp.broadcast_to(p[None], four)
    b = jnp.broadcast_to(b[None], four)
    y_start(NXP, pick(p, LANE - 1), pick(b, 0))
    onehots()

    def prepare_x():
        rate = rx[...]
        c = sums_x(rate, False)
        p, b = coefficients(cx, shape_of(rate), c, c[:, SUB - 1 :, :], sums_x_after)
        cx[6], f4, b4 = solve_x(ocean * ocean * cx[4])
        cx[7], f5, b5 = solve_x(ocean * ocean * cx[5])
        for k, (a, last) in enumerate(((p, 1), (b, 0), (f4, 1), (f5, 1), (b4, 0), (b5, 0))):
            buf = (ob, qb)[k % 2]
            put_rows(buf, jnp.stack([a] * TR))
            for j in range(nx):
                xcs[0, j, k * R : (k + 1) * R] = edge(buf, j, last)
        x_start(xcs, xcr, xc_ss, xc_rs, 0, xcs.shape[2])
        y_wait(NXP)

    def finish_x():
        x_wait(xcr, xc_ss, xc_rs, 0, xcs.shape[2])
        whole = xcr[0, 0, 0:R]
        for j in range(1, nx):
            whole = whole * xcr[0, j, 0:R]
        xinv[0:R] = 1.0 / (1.0 - whole)

    vals, _ = a_wait(0)
    y_start(0, *local_y(ocean * deposit(vals)))
    prepare_x()
    local_x(after_y(*y_finish(0)), True)
    finish_x()
    x_exchange(0, True)

    def begin():
        right = ocean * after_x()
        res[...] = right
        drn[...] = right
        return inner(right, right)

    back(1, begin)
    y, rr = a_wait(1)
    ydir[...] = y
    yres[...] = y
    dd = inner(drn[...], drn[...])
    for it in range(ITERS):
        last = it == ITERS - 1
        p = 2 * it + 2
        y = ydir[...]
        chunks = weigh(y)
        row = dd
        for k in range(nch):
            row = row + y[k] * chunks[k]
        a_start(p, chunks, row)
        if it > 0:
            drn[...] = res[...] + beta * drn[...]
        alpha = rr / forth(p, not last)

        sums = []

        def update():
            d = drn[...]
            sol[...] = alpha * d if it == 0 else sol[...] + alpha * d
            new = res[...] - alpha * (d + ocean * after_x())
            res[...] = new
            if last:
                return None
            own = inner(new, new)
            sums.extend((own, inner(new, d)))
            return own

        if last:
            update()
        else:
            back(p + 1, update)
            t, new_rr = a_wait(p + 1)
            beta = new_rr / rr
            rr = new_rr
            y = yres[...] - alpha * (ydir[...] + t)
            yres[...] = y
            ydir[...] = y + beta * ydir[...]
            dd = sums[0] + 2.0 * beta * sums[1] + beta * beta * dd


def on_device(nx, ny, rate_x, rate_y, land_mask, obs_cell, obs_count, innovation, obs_weight):
    lev, sx, sy = rate_x.shape
    slots = obs_cell.shape[2]
    nodes = nx * ny
    nch = nodes * slots // LANE
    lines = TR * lev
    assert (sx, sy) == (SUB, LANE) and lines % nx == 0 and lines <= LANE and LANE % slots == 0
    R = lines // nx
    M = (4 * R + 7) // 8 * 8
    MC = (6 * R + 7) // 8 * 8
    NXP = 2 * ITERS + 1
    field = (TR, lev, SUB, LANE)
    one = (lev, SUB, LANE)
    vm = pltpu.VMEM
    dma = pltpu.SemaphoreType.DMA
    Rp = (R + 7) // 8 * 8
    nb, rb = obs_weight.shape[1:3]
    return pl.pallas_call(
        functools.partial(kernel, nx, ny, lev, slots),
        out_shape=(jax.ShapeDtypeStruct(field, F32),) * 2,
        in_specs=[pl.BlockSpec(memory_space=vm)] * 7,
        out_specs=(pl.BlockSpec(memory_space=vm),) * 2,
        scratch_shapes=[
            vm(field, F32), vm(field, F32), vm(field, F32), vm(field, F32),
            vm((lines * SUB, LANE), F32), vm((lines * SUB, LANE), F32),
            vm((lines * SUB, LANE), F32), vm((lines * SUB, LANE), F32),
            vm((8,) + one, F32), vm((6,) + one, F32), vm((2, 3 * LANE, LANE), BF16),
            vm((nb, 3, rb, rb), BF16),
            vm((4, lines, LANE), F32),
            vm((lines * SUB, nch * LANE), BF16), vm((LANE, nch * LANE), F32),
            vm((nch, 1, LANE), F32), vm((nch, 1, LANE), F32), vm((nch, 1, LANE), F32),
            vm((Rp, LANE), F32),
            vm((NXP, nch, 2, LANE), F32), vm((NXP, nodes, 2, LANE), F32),
            vm((NXP, nx, M, LANE), F32), vm((NXP, nx, M, LANE), F32),
            vm((NXP, nx, M, LANE), F32), vm((NXP, nx, M, LANE), F32),
            vm((1, nx, MC, LANE), F32), vm((1, nx, MC, LANE), F32),
            vm((NXP + 1, 2 * SUB, LANE), F32), vm((NXP + 1, ny, 2 * SUB, LANE), F32),
            dma((NXP,)), dma((NXP,)), dma((NXP,)), dma((NXP,)), dma((NXP,)), dma((NXP,)),
            dma((1,)), dma((1,)), dma((NXP + 1,)), dma((NXP + 1,)),
        ],
        compiler_params=pltpu.CompilerParams(
            collective_id=0, has_side_effects=True, vmem_limit_bytes=56 * 1024 * 1024
        ),
    )(rate_x, rate_y, land_mask, obs_cell, obs_count, innovation, obs_weight)


def solution(mesh):
    placed = (
        P(None, "gx", "gy"),
        P(None, "gx", "gy"),
        P("gx", "gy"),
        P(("gx", "gy"), None, None),
        P(("gx", "gy"), None),
        P(("gx", "gy"), None, None),
        P(("gx", "gy"), None, None, None),
    )
    return jax.shard_map(
        functools.partial(on_device, mesh.shape["gx"], mesh.shape["gy"]),
        mesh=mesh,
        in_specs=placed,
        out_specs=(P(None, None, "gx", "gy"), P(None, None, "gx", "gy")),
        check_vma=False,
    )
```
